256 devices in a mesh: cfg: 2 (over y_hi), pipe: 8 (over z), seq: 16 (over x, y_lo, core).
Axes of the slice: x: 4, y: 4 (y_hi: 2, y_lo: 2; y = y_hi * 2 + y_lo), z: 8, core: 2. Of those that a mesh axis runs over, the one named last changes fastest.
Arguments:
- hidden: bfloat16 [2, 512, 4096], P('cfg', 'seq'), may hold values from -6 to 6
- modulation: float32 [8, 3, 4096], P('pipe'), may hold values from -24 to 24
- qkv_weight: bfloat16 [8, 3, 4096, 4096], P('pipe', None, None, 'seq'), may hold values from -4 to 4
- stale_cache: bfloat16 [2, 8, 2, 512, 4096], P('cfg', 'pipe', None, None, 'seq'), may hold values from -6 to 6
- patch_of: int32 [512], P('seq'), may hold values from 0 to 3, as said below
Outputs:
- guided: bfloat16 [512, 4096], P('seq', ('cfg', 'pipe'))
The draws below stay inside these ranges and needn't reach their ends.
Inputs may be any that keep to these rules, and one draw needn't show every extreme that they name: `patch_of`: each index of seq holds exactly 8 tokens of every patch.
All inputs are finite; a program needn't handle non-finite values.
Results may differ from the reference program's by a relative error of at most 0.035.
Values may be sent and summed in bfloat16 or wider, within the bound.
A program may use at most 64 MiB of HBM per device.

```python
import jax
import jax.numpy as jnp
from jax import lax

HEADS = 32
HD = 128
D = 4096
MICRO = 4
TOK_DEV = 32
TOKENS = 512
LAYERS = 8


def draw_modulation(key, part):
    key = jax.random.fold_in(key, 7)
    keys = jax.random.split(key, 3)
    shape = (LAYERS, D)
    shift = 0.5 * jax.random.normal(keys[0], shape, jnp.float32)
    scale = 0.3 * jax.random.normal(keys[1], shape, jnp.float32)
    gate = 0.6 * jax.random.normal(keys[2], shape, jnp.float32)
    stacked = jnp.stack([shift, scale, gate], axis=1)
    return jnp.clip(stacked, -24.0, 24.0).astype(jnp.float32)


def draw_qkv_weight(key, part):
    key = jax.random.fold_in(key, 5)
    keys = jax.random.split(key, 3)
    shape = (LAYERS, D, D)
    spread = 1.0 / jnp.sqrt(jnp.float32(D))
    query_w = spread * jax.random.normal(keys[0], shape, jnp.float32)
    key_w = spread * jax.random.normal(keys[1], shape, jnp.float32)
    value_w = spread * jax.random.normal(keys[2], shape, jnp.float32)
    stacked = jnp.stack([query_w, key_w, value_w], axis=1)
    return jnp.clip(stacked, -4.0, 4.0).astype(jnp.bfloat16)


def draw_patch_of(key, part):
    key = jax.random.fold_in(key, 11)
    block_count = TOKENS // TOK_DEV
    base_ids = jnp.arange(TOK_DEV, dtype=jnp.int32) // (TOK_DEV // MICRO)
    block_keys = jax.random.split(key, block_count)
    shuffled = jax.vmap(lambda block_key: jax.random.permutation(block_key, base_ids))(block_keys)
    return shuffled.reshape(TOKENS).astype(jnp.int32)


def block_levels(rng, shape, pieces, least, largest):
    gain = 1.0
    for position, parts in pieces:
        heights = jax.random.uniform(jax.random.fold_in(jax.random.fold_in(rng, 6), position), (parts,), jnp.float32, least / len(pieces), largest / len(pieces))
        gain = gain * jnp.repeat(jnp.exp(heights), shape[position] // parts).reshape((-1,) + (1,) * (len(shape) - 1 - position))
    return gain


def centred(stream_key, shape, scale, limit, shards=(), kind=jnp.bfloat16):
    entries = jax.random.normal(stream_key, shape, jnp.float32) * scale
    if len(shards) > 0:
        entries = block_levels(stream_key, shape, shards, -0.22, 0.18) * entries
    return jnp.clip(entries, min=-limit, max=limit).astype(kind)


def setup_inputs(seed: int = 0) -> dict:
    key_list = jax.random.split(jax.random.key(seed), 6)
    return {
        "hidden": centred(key_list[0], (2, TOKENS, D), 1.0, 6.0, ((0, 2), (1, 16))),
        "modulation": draw_modulation(jax.random.fold_in(key_list[5], 71), 0),
        "qkv_weight": draw_qkv_weight(jax.random.fold_in(key_list[5], 71), 0),
        "stale_cache": centred(key_list[3], (2, LAYERS, 2, TOKENS, D), 1.0, 6.0, ((0, 2), (1, 8), (4, 16))),
        "patch_of": draw_patch_of(jax.random.fold_in(key_list[5], 71), 0),
    }


GUIDANCE = 5.0
NORM_EPS = 1e-06

def norm_rows(x_float, shift, scale):
    row_mean = lax.optimization_barrier(jnp.mean(x_float, axis=-1, keepdims=True))
    row_var = lax.optimization_barrier(jnp.mean(x_float * x_float, axis=-1, keepdims=True)) - row_mean * row_mean
    return (x_float - row_mean) * lax.rsqrt(row_var + NORM_EPS) * (1.0 + scale) + shift

def head_slice(array, head):
    return lax.dynamic_slice_in_dim(array, head * HD, HD, 1)

def one_layer(x_rows, gains, weights, stale_rows, patch_of):
    x_float = x_rows.astype(jnp.float32)
    normed = norm_rows(x_float, gains[0], gains[1]).astype(jnp.bfloat16)
    query_rows = jnp.dot(normed, weights[0], preferred_element_type=jnp.float32).astype(jnp.bfloat16)
    key_rows = jnp.dot(normed, weights[1], preferred_element_type=jnp.float32).astype(jnp.bfloat16)
    value_rows = jnp.dot(normed, weights[2], preferred_element_type=jnp.float32).astype(jnp.bfloat16)
    later = patch_of[None, :] > patch_of[:, None]
    scaling = 1.0 / jnp.sqrt(jnp.float32(HD))

    def per_head(head):
        query_head = head_slice(query_rows, head)
        fresh_scores = jnp.dot(query_head, head_slice(key_rows, head).T, preferred_element_type=jnp.float32)
        stale_scores = jnp.dot(query_head, head_slice(stale_rows[0], head).T, preferred_element_type=jnp.float32)
        scores = jnp.where(later, stale_scores, fresh_scores) * scaling
        weights_soft = jax.nn.softmax(scores, axis=-1).astype(jnp.bfloat16)
        zero_weights = jnp.zeros_like(weights_soft)
        fresh_part = jnp.dot(jnp.where(later, zero_weights, weights_soft), head_slice(value_rows, head), preferred_element_type=jnp.float32)
        stale_part = jnp.dot(jnp.where(later, weights_soft, zero_weights), head_slice(stale_rows[1], head), preferred_element_type=jnp.float32)
        return fresh_part + stale_part
    per_heads = lax.map(per_head, jnp.arange(HEADS, dtype=jnp.int32))
    attended = jnp.transpose(per_heads, (1, 0, 2)).reshape(x_rows.shape[0], HEADS * HD).astype(jnp.bfloat16)
    return (x_float + gains[2] * attended.astype(jnp.float32)).astype(jnp.bfloat16)

def reference(hidden, modulation, qkv_weight, stale_cache, patch_of):
    finals = []
    for branch_index in range(2):
        x_rows = hidden[branch_index]
        for layer_index in range(LAYERS):
            x_rows = one_layer(x_rows, modulation[layer_index], qkv_weight[layer_index], stale_cache[branch_index, layer_index], patch_of)
        finals.append(x_rows.astype(jnp.float32))
    cond_pred = finals[0]
    uncond_pred = finals[1]
    return (uncond_pred + GUIDANCE * (cond_pred - uncond_pred)).astype(jnp.bfloat16)
```

```python
import functools

import jax
import jax.numpy as jnp
from jax import lax
from jax.experimental import pallas as pl
from jax.experimental.pallas import tpu as pltpu
from jax.sharding import PartitionSpec as P

F32 = jnp.float32
BF16 = jnp.bfloat16
MESH = pl.DeviceIdType.MESH

HD = 128
D = 4096
MICRO = 4
ROWS = 128
COLS = 256
SEQ = 16
PIPE = 8
GUIDANCE = 5.0
NORM_EPS = 1e-06

DIRECT = ((0, 0), (0, 1), (2, 0), (2, 1))
RELAY = ((1, 0), (3, 0), (1, 1), (3, 1))
OTHERS = DIRECT[1:] + RELAY
N_PLANE = len(OTHERS)
OWN_SIB = N_PLANE
FWD = OWN_SIB + 1
NEXT = FWD + N_PLANE
N_SEND = NEXT + len(DIRECT)
CHUNKS = 2
CW = COLS // CHUNKS


def kernel(
    hid_hbm, mod_hbm, w_hbm, stale_hbm, patch_ref, out_ref,
    x_buf, w_buf, hid, mod, stale, sorted_rows, kv, acc, sum1, sum2, colsum, shifted,
    pos_buf, x_out, fin_out, fin_in,
    load_sem, w_sem, pos_send, pos_recv, send_sem, recv_sem, fin_send, fin_recv,
):
    c = lax.axis_index("cfg")
    s = lax.axis_index("pipe")
    i = lax.axis_index("seq")
    core = i % 2
    y = (i // 2) % 2
    x = i // 4
    is_first = s == 0
    is_last = s == PIPE - 1

    def at(off, other=0):
        return (((x + off[0]) % 4) * 2 + (y + off[1]) % 2) * 2 + (core + other) % 2

    sib = at((0, 0), 1)
    out_col = c * PIPE + s

    loads = [
        pltpu.make_async_copy(hid_hbm.at[0], hid, load_sem.at[0]),
        pltpu.make_async_copy(mod_hbm.at[0], mod, load_sem.at[1]),
        pltpu.make_async_copy(stale_hbm.at[0, 0], stale, load_sem.at[2]),
    ]

    def w_copy(b):
        return pltpu.make_async_copy(
            w_hbm.at[0, :, pl.ds(pl.multiple_of(b * COLS, COLS), COLS), :], w_buf.at[b], w_sem.at[b]
        )

    barrier = pltpu.get_barrier_semaphore()

    def greet(target):
        pl.semaphore_signal(barrier, inc=1, device_id=target, device_id_type=MESH)

    def greet_plane(k, carry):
        greet((c, s, (i + k) % SEQ))
        return carry

    lax.fori_loop(1, SEQ, greet_plane, 0)

    @pl.when(s > 0)
    def _():
        for off in DIRECT:
            greet((c, s - 1, at(off)))

    for branch in range(2):
        is_self = jnp.logical_and(jnp.logical_and(c == branch, is_last), i == out_col)

        @pl.when(jnp.logical_not(is_self))
        def _():
            greet((branch, PIPE - 1, out_col))

    for load in loads:
        load.start()

    def start_w(b, carry):
        w_copy(b).start()
        return carry

    lax.fori_loop(0, SEQ, start_w, 0)

    patch_row = jnp.broadcast_to(patch_ref[...].astype(F32), (32, 32))
    row32 = lax.broadcasted_iota(jnp.int32, (32, 32), 0)
    col32 = lax.broadcasted_iota(jnp.int32, (32, 32), 1)
    patch_col = jnp.sum(jnp.where(row32 == col32, patch_row, 0.0), axis=1, keepdims=True)
    same = jnp.where(patch_row == patch_col, 1.0, 0.0)
    rank_col = jnp.sum(jnp.where(col32 < row32, same, 0.0), axis=1, keepdims=True)
    rank_row = jnp.sum(jnp.where(row32 < col32, same, 0.0), axis=0, keepdims=True)
    pos_row = patch_row[0:1] * 8.0 + rank_row
    pos_col = patch_col * 8.0 + rank_col
    to_sorted = jnp.where(pos_row == row32.astype(F32), 1.0, 0.0).astype(BF16)
    from_sorted = jnp.where(pos_col == col32.astype(F32), 1.0, 0.0).astype(BF16)
    whole_pos = patch_col * float(ROWS) + rank_col + (i * 8).astype(F32)
    row128 = lax.broadcasted_iota(jnp.int32, (32, 128), 0)
    lane128 = lax.broadcasted_iota(jnp.int32, (32, 128), 1)
    placed = jnp.where(lane128 == row128 + (i % 4) * 32, whole_pos, 0.0)
    pos_buf[i] = jnp.broadcast_to(jnp.sum(placed, axis=0, keepdims=True), (8, 128))

    is_own_out = jnp.logical_and(is_last, i == out_col)
    expected = (
        (SEQ - 1)
        + jnp.where(is_last, SEQ, len(DIRECT))
        - jnp.where(is_own_out, 1, 0)
    )
    pl.semaphore_wait(barrier, expected)

    def pos_copy(k):
        return pltpu.make_async_remote_copy(
            src_ref=pos_buf.at[i], dst_ref=pos_buf.at[i], send_sem=pos_send.at[k], recv_sem=pos_recv.at[i],
            device_id=(c, s, (i + k) % SEQ), device_id_type=MESH,
        )

    def pos_arrival(b):
        return pltpu.make_async_remote_copy(
            src_ref=pos_buf.at[b], dst_ref=pos_buf.at[b], send_sem=pos_send.at[0], recv_sem=pos_recv.at[b],
            device_id=(c, s, sib), device_id_type=MESH,
        )

    def slot_of(m):
        return m + jnp.where(is_first, MICRO, 0)

    def block_copy(m, b, k, number, target, slot):
        return pltpu.make_async_remote_copy(
            src_ref=x_buf.at[slot, b, k], dst_ref=x_buf.at[slot, b, k],
            send_sem=send_sem.at[m, number, k], recv_sem=recv_sem.at[m, b, k],
            device_id=(c, s, target), device_id_type=MESH,
        )

    def next_copy(m, k, n):
        return pltpu.make_async_remote_copy(
            src_ref=x_out.at[m, k], dst_ref=x_buf.at[m, i, k],
            send_sem=send_sem.at[m, NEXT + n, k], recv_sem=recv_sem.at[m, i, k],
            device_id=(c, s + 1, at(DIRECT[n])), device_id_type=MESH,
        )

    def arrive(m, b, k):
        block_copy(m, b, k, 0, sib, slot_of(m)).wait_recv()

    def spread_own(m):
        slot = slot_of(m)
        for k in range(CHUNKS):
            @pl.when(s > 0)
            def _():
                arrive(m, i, k)

            for n, off in enumerate(OTHERS):
                if off in RELAY:
                    block_copy(m, i, k, n, at(off), slot).start()
                else:
                    @pl.when(is_first)
                    def _():
                        block_copy(m, i, k, n, at(off), slot).start()

            block_copy(m, i, k, OWN_SIB, sib, slot).start()

    def take(m, number):
        b = at(OTHERS[number])
        for k in range(CHUNKS):
            arrive(m, b, k)
            block_copy(m, b, k, FWD + number, sib, slot_of(m)).start()

    @pl.when(is_first)
    def _():
        loads[0].wait()
        sorted_rows[...] = jnp.dot(to_sorted, hid[...], preferred_element_type=F32)
        for m in range(MICRO):
            for k in range(CHUNKS):
                pieces = [
                    sorted_rows[8 * m : 8 * m + 8, COLS * j + CW * k : COLS * j + CW * (k + 1)] for j in range(SEQ)
                ]
                x_buf[MICRO + m, i, k] = jnp.concatenate(pieces, axis=0).astype(BF16)
            if m == 0:
                spread_own(0)

    @pl.when(s > 0)
    def _():
        loads[0].wait()

    def send_pos(k, carry):
        pos_copy(k).start()
        return carry

    lax.fori_loop(1, SEQ, send_pos, 0)

    loads[1].wait()
    colsum[...] = jnp.zeros_like(colsum)
    shifted[...] = jnp.zeros_like(shifted)

    def fold(b, carry):
        w_copy(b).wait()
        span = pl.ds(pl.multiple_of(b * COLS, COLS), COLS)
        gain = jnp.broadcast_to(1.0 + mod[1:2, span], (128, COLS)).T
        gain = jnp.concatenate([gain, gain], axis=1)
        shift = jnp.broadcast_to(mod[0:1, span], (8, COLS))
        shift_high = shift.astype(BF16)
        shift_low = (shift - shift_high.astype(F32)).astype(BF16)
        shift_both = jnp.concatenate([shift_high, shift_low], axis=0)
        ones = jnp.ones((8, COLS), BF16)
        for t in range(3):
            raw = w_buf[b, t]
            shifted[t] += jnp.dot(shift_both, raw, preferred_element_type=F32)
            scaled = (raw.astype(F32) * gain).astype(BF16)
            w_buf[b, t] = scaled
            colsum[t] += jnp.dot(ones, scaled, preferred_element_type=F32)
        return carry

    lax.fori_loop(0, SEQ, fold, 0)

    loads[2].wait()

    def wait_pos(k, carry):
        pos_arrival((i + k) % SEQ).wait_recv()
        return carry

    lax.fori_loop(1, SEQ, wait_pos, 0)
    pos_all = jnp.concatenate(
        [sum(pos_buf[4 * g + n, 0:1, :] for n in range(4)) for g in range(4)], axis=1
    )
    for g in range(4):
        rows = lax.broadcasted_iota(jnp.int32, (128, 512), 0).astype(F32) + float(128 * g)
        pick = jnp.where(pos_all == rows, 1.0, 0.0).astype(BF16)
        for t in range(2):
            kv[t, 128 * g : 128 * g + 128, :] = jnp.dot(
                pick, stale[t], preferred_element_type=F32
            ).astype(BF16)

    @pl.when(s > 0)
    def _():
        spread_own(0)

    def block(m, b):
        return jnp.concatenate([x_buf[m, b, k] for k in range(CHUNKS)], axis=1)

    def project(m, blocks, fresh):
        parts = [block(m, b) for b in blocks]
        for t in range(3):
            total = sum(
                jnp.dot(part, w_buf[b, t], preferred_element_type=F32) for part, b in zip(parts, blocks)
            )
            acc[t] = total if fresh else acc[t] + total
        one = jnp.zeros((ROWS, 128), F32) if fresh else sum1[...]
        two = jnp.zeros((ROWS, 128), F32) if fresh else sum2[...]
        for part in parts:
            wide = part.astype(F32)
            square = wide * wide
            one = one + wide[:, :128] + wide[:, 128:]
            two = two + square[:, :128] + square[:, 128:]
        sum1[...] = one
        sum2[...] = two

    scaling = 1.0 / (HD ** 0.5)

    def patch_step(m, carry):
        @pl.when(is_first)
        def _():
            for number in range(N_PLANE):
                take(m, number)
            for off in DIRECT + RELAY:
                for k in range(CHUNKS):
                    arrive(m, at(off, 1), k)

            def regroup(jj, inner):
                span = pl.ds(pl.multiple_of(jj * 16, 16), 16)
                for k in range(CHUNKS):
                    pieces = [x_buf[MICRO + m, b, k, span, :].astype(F32) for b in range(SEQ)]
                    for half in range(2):
                        x_buf[m, 2 * jj + half, k] = jnp.concatenate(
                            [piece[8 * half : 8 * half + 8] for piece in pieces], axis=0
                        ).astype(BF16)
                return inner

            lax.fori_loop(0, SEQ // 2, regroup, 0)

        n_direct = len(DIRECT) - 1

        @pl.when(s > 0)
        def _():
            for number in range(n_direct):
                take(m, number)

        project(m, [at(off) for off in DIRECT], True)

        @pl.when(s > 0)
        def _():
            for number in range(n_direct, N_PLANE):
                take(m, number)

        project(m, [at(off) for off in RELAY], False)

        for group in (DIRECT, RELAY):
            @pl.when(s > 0)
            def _():
                for off in group:
                    for k in range(CHUNKS):
                        arrive(m, at(off, 1), k)

            project(m, [at(off, 1) for off in group], False)

        @pl.when(m < MICRO - 1)
        def _():
            spread_own(m + 1)

        mean = jnp.sum(sum1[...], axis=1, keepdims=True) * (1.0 / D)
        var = jnp.sum(sum2[...], axis=1, keepdims=True) * (1.0 / D) - mean * mean
        inv = lax.rsqrt(var + NORM_EPS)

        def finish(t):
            bias = shifted[t, 0:1] + shifted[t, 8:9]
            return (inv * (acc[t] - mean * colsum[t, 0:1]) + bias).astype(BF16)

        query = finish(0)
        rows = pl.ds(pl.multiple_of(m * ROWS, ROWS), ROWS)
        kv[0, rows, :] = finish(1)
        kv[1, rows, :] = finish(2)
        own = pl.ds(pl.multiple_of(i * COLS, COLS), COLS)
        gate = mod[2:3, own]
        old = block(m, i)
        for h in range(2):
            cols = slice(h * HD, (h + 1) * HD)
            scores = lax.dot_general(
                query[:, cols], kv[0, :, cols], (((1,), (1,)), ((), ())), preferred_element_type=F32
            )
            top = jnp.max(scores, axis=1, keepdims=True)
            weights = jnp.exp((scores - top) * scaling)
            norm = jnp.sum(weights, axis=1, keepdims=True)
            mixed = jnp.dot(weights.astype(BF16), kv[1, :, cols], preferred_element_type=F32) / norm
            mixed = mixed.astype(BF16).astype(F32)
            fresh = (old[:, cols].astype(F32) + gate[:, cols] * mixed).astype(BF16)
            if CHUNKS == 2:
                x_out[m, h] = fresh
            else:
                x_out[m, 0, :, cols] = fresh
            if CHUNKS == 2 or h == 1:
                @pl.when(s < PIPE - 1)
                def _():
                    for n in range(len(DIRECT)):
                        next_copy(m, h if CHUNKS == 2 else 0, n).start()

        @pl.when(is_last)
        def _():
            done = jnp.concatenate([x_out[m, k] for k in range(CHUNKS)], axis=1).astype(F32)
            for b in range(SEQ):
                piece = done[8 * b : 8 * b + 8]
                fin_out[m, b] = jnp.concatenate([piece[:, :128], piece[:, 128:]], axis=0).astype(BF16)
            for b in range(SEQ):
                goes_home = jnp.logical_and(is_own_out, i == b)

                @pl.when(goes_home)
                def _():
                    home_copy(m, b).start()

                @pl.when(jnp.logical_not(goes_home))
                def _():
                    fin_copy(m, b).start()

        return carry

    def fin_copy(m, b):
        return pltpu.make_async_remote_copy(
            src_ref=fin_out.at[m, b], dst_ref=fin_in.at[c, m], send_sem=fin_send.at[m, b], recv_sem=fin_recv.at[c, m],
            device_id=(i // PIPE, i % PIPE, b), device_id_type=MESH,
        )

    def home_copy(m, b):
        return pltpu.make_async_copy(fin_out.at[m, b], fin_in.at[c, m], fin_recv.at[c, m])

    lax.fori_loop(0, MICRO, patch_step, 0)

    def drain_pos(k, carry):
        pos_copy(k).wait_send()
        return carry

    lax.fori_loop(1, SEQ, drain_pos, 0)

    def drain(m, carry):
        slot = slot_of(m)
        for k in range(CHUNKS):
            for n, off in enumerate(OTHERS):
                if off in RELAY:
                    block_copy(m, i, k, n, at(off), slot).wait_send()
                else:
                    @pl.when(is_first)
                    def _():
                        block_copy(m, i, k, n, at(off), slot).wait_send()
                block_copy(m, at(off), k, FWD + n, sib, slot).wait_send()
            block_copy(m, i, k, OWN_SIB, sib, slot).wait_send()

            @pl.when(s < PIPE - 1)
            def _():
                for n in range(len(DIRECT)):
                    next_copy(m, k, n).wait_send()

        @pl.when(is_last)
        def _():
            for b in range(SEQ):
                @pl.when(jnp.logical_not(jnp.logical_and(is_own_out, i == b)))
                def _():
                    fin_copy(m, b).wait_send()

        return carry

    lax.fori_loop(0, MICRO, drain, 0)

    guided = []
    for m in range(MICRO):
        for branch in range(2):
            pltpu.make_async_remote_copy(
                src_ref=fin_out.at[m, 0], dst_ref=fin_in.at[branch, m], send_sem=fin_send.at[0, 0],
                recv_sem=fin_recv.at[branch, m], device_id=(c, s, sib), device_id_type=MESH,
            ).wait_recv()
        cond = fin_in[0, m].astype(F32)
        uncond = fin_in[1, m].astype(F32)
        piece = uncond + GUIDANCE * (cond - uncond)
        guided.append(jnp.concatenate([piece[:8], piece[8:]], axis=1))
    guided = jnp.concatenate(guided, axis=0).astype(BF16)
    out_ref[...] = jnp.dot(from_sorted, guided, preferred_element_type=F32).astype(BF16)


def body(hidden, modulation, qkv_weight, stale_cache, patch_of):
    vmem, dma = pltpu.VMEM, pltpu.SemaphoreType.DMA
    hbm = pl.BlockSpec(memory_space=pl.ANY)
    return pl.pallas_call(
        kernel,
        out_shape=jax.ShapeDtypeStruct((32, COLS), BF16),
        in_specs=[hbm, hbm, hbm, hbm, pl.BlockSpec(memory_space=pltpu.VMEM)],
        out_specs=pl.BlockSpec(memory_space=pltpu.VMEM),
        scratch_shapes=[
            vmem((2 * MICRO, SEQ, CHUNKS, ROWS, CW), BF16),
            vmem((SEQ, 3, COLS, COLS), BF16),
            vmem((32, D), BF16),
            vmem((3, D), F32),
            vmem((2, 512, COLS), BF16),
            vmem((32, D), F32),
            vmem((2, 512, COLS), BF16),
            vmem((3, ROWS, COLS), F32),
            vmem((ROWS, 128), F32),
            vmem((ROWS, 128), F32),
            vmem((3, 8, COLS), F32),
            vmem((3, 16, COLS), F32),
            vmem((SEQ, 8, 128), F32),
            vmem((MICRO, CHUNKS, ROWS, CW), BF16),
            vmem((MICRO, SEQ, 16, 128), BF16),
            vmem((2, MICRO, 16, 128), BF16),
            dma((3,)),
            dma((SEQ,)),
            dma((SEQ,)),
            dma((SEQ,)),
            dma((MICRO, N_SEND, CHUNKS)),
            dma((MICRO, SEQ, CHUNKS)),
            dma((MICRO, SEQ)),
            dma((2, MICRO)),
        ],
        compiler_params=pltpu.CompilerParams(
            collective_id=0, has_side_effects=True, vmem_limit_bytes=40 * 2**20
        ),
        cost_estimate=pl.CostEstimate(flops=4 * 10**9, bytes_accessed=8 * 2**20, transcendentals=10**6),
        name="layers",
    )(hidden, modulation, qkv_weight, stale_cache, patch_of.reshape(1, 32))


def solution(mesh):
    placed = (
        P("cfg", "seq", None),
        P("pipe", None, None),
        P("pipe", None, None, "seq"),
        P("cfg", "pipe", None, None, "seq"),
        P("seq"),
    )
    return jax.shard_map(
        body, mesh=mesh, in_specs=placed, out_specs=P("seq", ("cfg", "pipe")), check_vma=False
    )
```

```python
import functools

import jax
import jax.numpy as jnp
from jax import lax
from jax.experimental import pallas as pl
from jax.experimental.pallas import tpu as pltpu
from jax.sharding import PartitionSpec as P

F32 = jnp.float32
BF16 = jnp.bfloat16
MESH = pl.DeviceIdType.MESH

HD = 128
D = 4096
MICRO = 4
ROWS = 128
COLS = 256
SEQ = 16
PIPE = 8
GUIDANCE = 5.0
NORM_EPS = 1e-06

OFFSETS = ((0, 0), (0, 1), (2, 0), (2, 1), (1, 0), (3, 0), (1, 1), (3, 1))
BACK = (0, 1, 2, 3, 5, 4, 7, 6)
CHIPS = 8
GROUPS = ((0, 1), (1, 4), (4, 8))
OWN, DIRECT, RELAY = 0, 1, 2
CHUNKS = 2
CW = COLS // CHUNKS


def kernel(
    hid_hbm, mod_hbm, w_hbm, stale_hbm, patch_ref, out_ref,
    x_buf, w_buf, hid, mod, stale, sorted_rows, kv, acc, sum1, sum2, colsum, shifted,
    pos_buf, x_out, fin_out, fin_in,
    load_sem, w_sem, pos_send, pos_recv, plane_sem, fwd_sem, next_sem, recv_sem, fin_send, fin_recv,
):
    c = lax.axis_index("cfg")
    s = lax.axis_index("pipe")
    i = lax.axis_index("seq")
    core = i % 2
    y = (i // 2) % 2
    x = i // 4
    is_first = s == 0
    is_last = s == PIPE - 1
    relay_flip = jnp.where(is_first, 0, 1)

    def at(n, other=0):
        dx, dy = OFFSETS[n]
        return (((x + dx) % 4) * 2 + (y + dy) % 2) * 2 + (core + other) % 2

    def source(side, n):
        return at(n, side + relay_flip if n >= GROUPS[RELAY][0] else side)

    sib = at(0, 1)
    out_col = c * PIPE + s

    loads = [
        pltpu.make_async_copy(hid_hbm.at[0], hid, load_sem.at[0]),
        pltpu.make_async_copy(mod_hbm, mod, load_sem.at[1]),
        pltpu.make_async_copy(stale_hbm.at[0, 0], stale, load_sem.at[2]),
    ]

    def w_copy(b):
        return pltpu.make_async_copy(
            w_hbm.at[0, :, pl.ds(pl.multiple_of(b * COLS, COLS), COLS), :], w_buf.at[b], w_sem.at[b]
        )

    barrier = pltpu.get_barrier_semaphore()

    def greet(target):
        pl.semaphore_signal(barrier, inc=1, device_id=target, device_id_type=MESH)

    def greet_plane(k, carry):
        greet((c, s, (i + k) % SEQ))
        return carry

    lax.fori_loop(1, SEQ, greet_plane, 0)

    @pl.when(s > 0)
    def _():
        for n in range(GROUPS[RELAY][0]):
            greet((c, s - 1, at(n)))

    for branch in range(2):
        is_self = jnp.logical_and(jnp.logical_and(c == branch, is_last), i == out_col)

        @pl.when(jnp.logical_not(is_self))
        def _():
            greet((branch, PIPE - 1, out_col))

    for load in loads:
        load.start()

    def start_w(b, carry):
        w_copy(b).start()
        return carry

    lax.fori_loop(0, SEQ, start_w, 0)

    patch_row = jnp.broadcast_to(patch_ref[...].astype(F32), (32, 32))
    row32 = lax.broadcasted_iota(jnp.int32, (32, 32), 0)
    col32 = lax.broadcasted_iota(jnp.int32, (32, 32), 1)
    patch_col = jnp.sum(jnp.where(row32 == col32, patch_row, 0.0), axis=1, keepdims=True)
    same = jnp.where(patch_row == patch_col, 1.0, 0.0)
    rank_col = jnp.sum(jnp.where(col32 < row32, same, 0.0), axis=1, keepdims=True)
    rank_row = jnp.sum(jnp.where(row32 < col32, same, 0.0), axis=0, keepdims=True)
    pos_row = patch_row[0:1] * 8.0 + rank_row
    pos_col = patch_col * 8.0 + rank_col
    to_sorted = jnp.where(pos_row == row32.astype(F32), 1.0, 0.0).astype(BF16)
    from_sorted = jnp.where(pos_col == col32.astype(F32), 1.0, 0.0).astype(BF16)
    whole_pos = patch_col * float(ROWS) + rank_col + (i * 8).astype(F32)
    row128 = lax.broadcasted_iota(jnp.int32, (32, 128), 0)
    lane128 = lax.broadcasted_iota(jnp.int32, (32, 128), 1)
    placed = jnp.where(lane128 == row128 + (i % 4) * 32, whole_pos, 0.0)
    pos_buf[i] = jnp.broadcast_to(jnp.sum(placed, axis=0, keepdims=True), (8, 128))

    @pl.when(is_first)
    def _():
        loads[0].wait()
        sorted_rows[...] = jnp.dot(to_sorted, hid[...], preferred_element_type=F32)
        for m in range(MICRO):
            for k in range(CHUNKS):
                pieces = [
                    sorted_rows[8 * m : 8 * m + 8, COLS * j + CW * k : COLS * j + CW * (k + 1)] for j in range(SEQ)
                ]
                x_buf[MICRO + m, 0, k, 0] = jnp.concatenate(pieces, axis=0).astype(BF16)

    @pl.when(s > 0)
    def _():
        loads[0].wait()

    is_own_out = jnp.logical_and(is_last, i == out_col)
    expected = (
        (SEQ - 1)
        + jnp.where(is_last, SEQ, GROUPS[RELAY][0])
        - jnp.where(is_own_out, 1, 0)
    )
    pl.semaphore_wait(barrier, expected)

    def pos_copy(k):
        return pltpu.make_async_remote_copy(
            src_ref=pos_buf.at[i], dst_ref=pos_buf.at[i], send_sem=pos_send.at[k], recv_sem=pos_recv.at[i],
            device_id=(c, s, (i + k) % SEQ), device_id_type=MESH,
        )

    def pos_arrival(b):
        return pltpu.make_async_remote_copy(
            src_ref=pos_buf.at[b], dst_ref=pos_buf.at[b], send_sem=pos_send.at[0], recv_sem=pos_recv.at[b],
            device_id=(c, s, sib), device_id_type=MESH,
        )

    def slot_of(m):
        return m + jnp.where(is_first, MICRO, 0)

    def remote(src, dst, send, recv, target):
        return pltpu.make_async_remote_copy(
            src_ref=src, dst_ref=dst, send_sem=send, recv_sem=recv, device_id=target, device_id_type=MESH
        )

    def region(m, side, k, group):
        low, high = GROUPS[group]
        return x_buf.at[slot_of(m), side, k, pl.ds(low, high - low)]

    def plane_copy(m, k, n, flip):
        slot = slot_of(m)
        return remote(
            x_buf.at[slot, 0, k, 0], x_buf.at[slot, 0, k, BACK[n]],
            plane_sem.at[m], recv_sem.at[m, 0, DIRECT if n < GROUPS[RELAY][0] else RELAY, k], (c, s, at(n, flip)),
        )

    def fwd_copy(m, k, group):
        return remote(
            region(m, 0, k, group), region(m, 1, k, group), fwd_sem.at[m], recv_sem.at[m, 1, group, k], (c, s, sib)
        )

    def next_copy(m, k, n):
        return remote(
            x_out.at[m, k], x_buf.at[m, 0, k, n],
            next_sem.at[m], recv_sem.at[m, 0, OWN if n == 0 else DIRECT, k], (c, s + 1, at(n)),
        )

    def arrive(m, side, k, group):
        here = region(m, side, k, group)
        remote(here, here, fwd_sem.at[m], recv_sem.at[m, side, group, k], (c, s, sib)).wait_recv()

    def take(m, group):
        for k in range(CHUNKS):
            arrive(m, 0, k, group)
            fwd_copy(m, k, group).start()

    def take_sib(m, *groups):
        for group in groups:
            for k in range(CHUNKS):
                arrive(m, 1, k, group)

    def spread_first(m):
        for n in range(1, CHIPS):
            for k in range(CHUNKS):
                plane_copy(m, k, n, 0).start()
        for k in range(CHUNKS):
            fwd_copy(m, k, OWN).start()

    def spread_relay(m):
        for k in range(CHUNKS):
            arrive(m, 0, k, OWN)
            for n in range(*GROUPS[RELAY]):
                plane_copy(m, k, n, 1).start()
            fwd_copy(m, k, OWN).start()

    @pl.when(is_first)
    def _():
        spread_first(0)

    def send_pos(k, carry):
        pos_copy(k).start()
        return carry

    lax.fori_loop(1, SEQ, send_pos, 0)

    loads[1].wait()
    colsum[...] = jnp.zeros_like(colsum)
    shifted[...] = jnp.zeros_like(shifted)

    def fold(b, carry):
        w_copy(b).wait()
        gain = jnp.concatenate(
            [jnp.broadcast_to(1.0 + mod[pl.ds(32 + 2 * b + n, 1), :], (128, 128)).T for n in range(2)], axis=0
        )
        gain = jnp.concatenate([gain, gain], axis=1)
        shift = jnp.broadcast_to(
            jnp.concatenate([mod[pl.ds(2 * b + n, 1), :] for n in range(2)], axis=1), (8, COLS)
        )
        shift_high = shift.astype(BF16)
        shift_low = (shift - shift_high.astype(F32)).astype(BF16)
        shift_both = jnp.concatenate([shift_high, shift_low], axis=0)
        ones = jnp.ones((8, COLS), BF16)
        for t in range(3):
            raw = w_buf[b, t]
            shifted[t] += jnp.dot(shift_both, raw, preferred_element_type=F32)
            scaled = (raw.astype(F32) * gain).astype(BF16)
            w_buf[b, t] = scaled
            colsum[t] += jnp.dot(ones, scaled, preferred_element_type=F32)
        return carry

    lax.fori_loop(0, SEQ // 2, fold, 0)

    @pl.when(is_first)
    def _():
        spread_first(1)

    lax.fori_loop(SEQ // 2, SEQ, fold, 0)

    loads[2].wait()

    def wait_pos(k, carry):
        pos_arrival((i + k) % SEQ).wait_recv()
        return carry

    lax.fori_loop(1, SEQ, wait_pos, 0)
    pos_all = jnp.concatenate(
        [sum(pos_buf[4 * g + n, 0:1, :] for n in range(4)) for g in range(4)], axis=1
    )
    for g in range(4):
        rows = lax.broadcasted_iota(jnp.int32, (128, 512), 0).astype(F32) + float(128 * g)
        pick = jnp.where(pos_all == rows, 1.0, 0.0).astype(BF16)
        for t in range(2):
            kv[t, 128 * g : 128 * g + 128, :] = jnp.dot(
                pick, stale[t], preferred_element_type=F32
            ).astype(BF16)

    @pl.when(s > 0)
    def _():
        spread_relay(0)

    def block(m, side, n):
        return jnp.concatenate([x_buf[m, side, k, n] for k in range(CHUNKS)], axis=1)

    def project(m, side, low, high):
        parts = [block(m, side, n) for n in range(low, high)]
        rows = [source(side, n) for n in range(low, high)]
        fresh = side == 0 and low == 0
        for t in range(3):
            total = sum(jnp.dot(part, w_buf[b, t], preferred_element_type=F32) for part, b in zip(parts, rows))
            acc[t] = total if fresh else acc[t] + total
        one = jnp.zeros((ROWS, 128), F32) if fresh else sum1[...]
        two = jnp.zeros((ROWS, 128), F32) if fresh else sum2[...]
        for part in parts:
            wide = part.astype(F32)
            square = wide * wide
            one = one + wide[:, :128] + wide[:, 128:]
            two = two + square[:, :128] + square[:, 128:]
        sum1[...] = one
        sum2[...] = two

    scaling = 1.0 / (HD ** 0.5)

    def patch_step(m, carry):
        @pl.when(is_first)
        def _():
            take(m, DIRECT)
            take(m, RELAY)
            take_sib(m, OWN, DIRECT, RELAY)

            @pl.when(m < MICRO - 2)
            def _():
                spread_first(m + 2)

            def where_is(b):
                dx = (b // 4 - x + 4) % 4
                dy = ((b // 2) % 2 - y + 2) % 2
                return (b + core) % 2, jnp.where(dx % 2 == 0, dx + dy, 4 + 2 * dy + dx // 2)

            homes = [where_is(b) for b in range(SEQ)]
            for n in range(CHIPS):
                span = pl.ds(pl.multiple_of((at(n) // 2) * 16, 16), 16)
                for k in range(CHUNKS):
                    pieces = [x_buf[MICRO + m, side, k, chip, span, :].astype(F32) for side, chip in homes]
                    for half in range(2):
                        x_buf[m, (half + core) % 2, k, n] = jnp.concatenate(
                            [piece[8 * half : 8 * half + 8] for piece in pieces], axis=0
                        ).astype(BF16)

        @pl.when(s > 0)
        def _():
            take(m, DIRECT)

        project(m, 0, 0, 4)

        @pl.when(s > 0)
        def _():
            take_sib(m, OWN, DIRECT)

        project(m, 1, 0, 4)

        @pl.when(s > 0)
        def _():
            take(m, RELAY)

            @pl.when(m < MICRO - 1)
            def _():
                spread_relay(m + 1)

        project(m, 0, 4, 8)

        @pl.when(s > 0)
        def _():
            take_sib(m, RELAY)

        project(m, 1, 4, 8)

        mean = jnp.sum(sum1[...], axis=1, keepdims=True) * (1.0 / D)
        var = jnp.sum(sum2[...], axis=1, keepdims=True) * (1.0 / D) - mean * mean
        inv = lax.rsqrt(var + NORM_EPS)

        def finish(t):
            bias = shifted[t, 0:1] + shifted[t, 8:9]
            return (inv * (acc[t] - mean * colsum[t, 0:1]) + bias).astype(BF16)

        query = finish(0)
        rows = pl.ds(pl.multiple_of(m * ROWS, ROWS), ROWS)
        kv[0, rows, :] = finish(1)
        kv[1, rows, :] = finish(2)
        old = block(m, 0, 0)
        for h in range(2):
            cols = slice(h * HD, (h + 1) * HD)
            scores = lax.dot_general(
                query[:, cols], kv[0, :, cols], (((1,), (1,)), ((), ())), preferred_element_type=F32
            )
            top = jnp.max(scores, axis=1, keepdims=True)
            weights = jnp.exp((scores - top) * scaling)
            norm = jnp.sum(weights, axis=1, keepdims=True)
            mixed = jnp.dot(weights.astype(BF16), kv[1, :, cols], preferred_element_type=F32) / norm
            mixed = mixed.astype(BF16).astype(F32)
            fresh = (old[:, cols].astype(F32) + mod[pl.ds(64 + 2 * i + h, 1), :] * mixed).astype(BF16)
            x_out[m, h] = fresh

            @pl.when(s < PIPE - 1)
            def _():
                next_copy(m, h, 0).start()
                if h == 1:
                    for k in range(CHUNKS):
                        for n in range(1, GROUPS[RELAY][0]):
                            next_copy(m, k, n).start()

        @pl.when(is_last)
        def _():
            done = jnp.concatenate([x_out[m, k] for k in range(CHUNKS)], axis=1).astype(F32)
            for b in range(SEQ):
                piece = done[8 * b : 8 * b + 8]
                fin_out[m, b] = jnp.concatenate([piece[:, :128], piece[:, 128:]], axis=0).astype(BF16)

            @pl.when(is_own_out)
            def _():
                home_copy(m).start()

                def send(k, inner):
                    fin_copy(m, (i + k) % SEQ).start()
                    return inner

                lax.fori_loop(1, SEQ, send, 0)

            @pl.when(jnp.logical_not(is_own_out))
            def _():
                for b in range(SEQ):
                    fin_copy(m, b).start()

        return carry

    def fin_copy(m, b):
        return remote(
            fin_out.at[m, b], fin_in.at[c, m], fin_send.at[m], fin_recv.at[c, m], (i // PIPE, i % PIPE, b)
        )

    def home_copy(m):
        return pltpu.make_async_copy(fin_out.at[m, i], fin_in.at[c, m], fin_recv.at[c, m])

    lax.fori_loop(0, MICRO, patch_step, 0)

    def left(ref, sem):
        remote(ref, ref, sem, recv_sem.at[0, 0, 0, 0], (c, s, sib)).wait_send()

    def drain_pos(k, carry):
        pos_copy(k).wait_send()
        return carry

    lax.fori_loop(1, SEQ, drain_pos, 0)

    for m in range(MICRO):
        left(x_buf.at[0, 0], fwd_sem.at[m])

        @pl.when(is_first)
        def _():
            left(x_buf.at[0, 0, :, pl.ds(0, 7)], plane_sem.at[m])

        @pl.when(s > 0)
        def _():
            left(x_buf.at[0, 0, 0], plane_sem.at[m])

        @pl.when(s < PIPE - 1)
        def _():
            left(x_buf.at[0, 0, 0], next_sem.at[m])

        @pl.when(jnp.logical_and(is_last, is_own_out))
        def _():
            left(fin_out.at[m, pl.ds(0, SEQ - 1)], fin_send.at[m])

        @pl.when(jnp.logical_and(is_last, jnp.logical_not(is_own_out)))
        def _():
            left(fin_out.at[m], fin_send.at[m])

    guided = []
    for m in range(MICRO):
        for branch in range(2):
            here = fin_in.at[branch, m]
            remote(here, here, fin_send.at[m], fin_recv.at[branch, m], (c, s, sib)).wait_recv()
        cond = fin_in[0, m].astype(F32)
        uncond = fin_in[1, m].astype(F32)
        piece = uncond + GUIDANCE * (cond - uncond)
        guided.append(jnp.concatenate([piece[:8], piece[8:]], axis=1))
    guided = jnp.concatenate(guided, axis=0).astype(BF16)
    out_ref[...] = jnp.dot(from_sorted, guided, preferred_element_type=F32).astype(BF16)


def body(hidden, modulation, qkv_weight, stale_cache, patch_of):
    vmem, dma = pltpu.VMEM, pltpu.SemaphoreType.DMA
    hbm = pl.BlockSpec(memory_space=pl.ANY)
    return pl.pallas_call(
        kernel,
        out_shape=jax.ShapeDtypeStruct((32, COLS), BF16),
        in_specs=[hbm, hbm, hbm, hbm, pl.BlockSpec(memory_space=pltpu.VMEM)],
        out_specs=pl.BlockSpec(memory_space=pltpu.VMEM),
        scratch_shapes=[
            vmem((2 * MICRO, 2, CHUNKS, CHIPS, ROWS, CW), BF16),
            vmem((SEQ, 3, COLS, COLS), BF16),
            vmem((32, D), BF16),
            vmem((96, 128), F32),
            vmem((2, 512, COLS), BF16),
            vmem((32, D), F32),
            vmem((2, 512, COLS), BF16),
            vmem((3, ROWS, COLS), F32),
            vmem((ROWS, 128), F32),
            vmem((ROWS, 128), F32),
            vmem((3, 8, COLS), F32),
            vmem((3, 16, COLS), F32),
            vmem((SEQ, 8, 128), F32),
            vmem((MICRO, CHUNKS, ROWS, CW), BF16),
            vmem((MICRO, SEQ, 16, 128), BF16),
            vmem((2, MICRO, 16, 128), BF16),
            dma((3,)),
            dma((SEQ,)),
            dma((SEQ,)),
            dma((SEQ,)),
            dma((MICRO,)),
            dma((MICRO,)),
            dma((MICRO,)),
            dma((MICRO, 2, 3, CHUNKS)),
            dma((MICRO,)),
            dma((2, MICRO)),
        ],
        compiler_params=pltpu.CompilerParams(
            collective_id=0, has_side_effects=True, vmem_limit_bytes=56 * 2**20
        ),
        cost_estimate=pl.CostEstimate(flops=4 * 10**9, bytes_accessed=8 * 2**20, transcendentals=10**6),
        name="layers",
    )(hidden, modulation.reshape(96, 128), qkv_weight, stale_cache, patch_of.reshape(1, 32))


def solution(mesh):
    placed = (
        P("cfg", "seq", None),
        P("pipe", None, None),
        P("pipe", None, None, "seq"),
        P("cfg", "pipe", None, None, "seq"),
        P("seq"),
    )
    return jax.shard_map(
        body, mesh=mesh, in_specs=placed, out_specs=P("seq", ("cfg", "pipe")), check_vma=False
    )
```

```python
import functools

import jax
import jax.numpy as jnp
from jax import lax
from jax.experimental import pallas as pl
from jax.experimental.pallas import tpu as pltpu
from jax.sharding import PartitionSpec as P

F32 = jnp.float32
BF16 = jnp.bfloat16
MESH = pl.DeviceIdType.MESH

HD = 128
D = 4096
MICRO = 4
ROWS = 128
COLS = 256
SEQ = 16
PIPE = 8
GUIDANCE = 5.0
NORM_EPS = 1e-06

OFFSETS = ((0, 0), (1, 1), (3, 1), (2, 1), (1, 0), (3, 0), (2, 0), (0, 1))
BACK = tuple(OFFSETS.index(((4 - dx) % 4, dy)) for dx, dy in OFFSETS)
CHIPS = 8
N_DIRECT = 4
GROUPS = ((0, 1), (1, N_DIRECT), (N_DIRECT, CHIPS))
OWN, DIRECT, RELAY = 0, 1, 2
CHUNKS = 2
CW = COLS // CHUNKS


def kernel(
    hid_hbm, mod_hbm, w_hbm, stale_hbm, patch_ref, out_ref,
    x_buf, w_buf, hid, mod, stale, sorted_rows, kv, acc, sum1, sum2, colsum, shifted,
    pos_buf, x_out, fin_out, fin_in,
    load_sem, w_sem, pos_send, pos_recv, plane_sem, fwd_sem, next_sem, recv_sem, fin_send, fin_recv,
):
    c = lax.axis_index("cfg")
    s = lax.axis_index("pipe")
    i = lax.axis_index("seq")
    core = i % 2
    y = (i // 2) % 2
    x = i // 4
    is_first = s == 0
    is_last = s == PIPE - 1
    relay_flip = jnp.where(is_first, 0, 1)

    def at(n, other=0):
        dx, dy = OFFSETS[n]
        return (((x + dx) % 4) * 2 + (y + dy) % 2) * 2 + (core + other) % 2

    def source(side, n):
        return at(n, side + relay_flip if n >= N_DIRECT else side)

    sib = at(0, 1)
    out_col = c * PIPE + s

    loads = [
        pltpu.make_async_copy(hid_hbm.at[0], hid, load_sem.at[0]),
        pltpu.make_async_copy(mod_hbm, mod, load_sem.at[1]),
        pltpu.make_async_copy(stale_hbm.at[0, 0], stale, load_sem.at[2]),
    ]

    def w_copy(b):
        return pltpu.make_async_copy(
            w_hbm.at[0, :, pl.ds(pl.multiple_of(b * COLS, COLS), COLS), :], w_buf.at[b], w_sem.at[b]
        )

    barrier = pltpu.get_barrier_semaphore()

    def greet(target):
        pl.semaphore_signal(barrier, inc=1, device_id=target, device_id_type=MESH)

    def greet_plane(k, carry):
        greet((c, s, (i + k) % SEQ))
        return carry

    lax.fori_loop(1, SEQ, greet_plane, 0)

    @pl.when(s > 0)
    def _():
        for n in range(N_DIRECT):
            greet((c, s - 1, at(n)))

    for branch in range(2):
        is_self = jnp.logical_and(jnp.logical_and(c == branch, is_last), i == out_col)

        @pl.when(jnp.logical_not(is_self))
        def _():
            greet((branch, PIPE - 1, out_col))

    for load in loads:
        load.start()

    def start_w(b, carry):
        w_copy(b).start()
        return carry

    patch_row = jnp.broadcast_to(patch_ref[...].astype(F32), (32, 32))
    row32 = lax.broadcasted_iota(jnp.int32, (32, 32), 0)
    col32 = lax.broadcasted_iota(jnp.int32, (32, 32), 1)
    patch_col = jnp.sum(jnp.where(row32 == col32, patch_row, 0.0), axis=1, keepdims=True)
    same = jnp.where(patch_row == patch_col, 1.0, 0.0)
    rank_col = jnp.sum(jnp.where(col32 < row32, same, 0.0), axis=1, keepdims=True)
    rank_row = jnp.sum(jnp.where(row32 < col32, same, 0.0), axis=0, keepdims=True)
    pos_row = patch_row[0:1] * 8.0 + rank_row
    pos_col = patch_col * 8.0 + rank_col
    to_sorted = jnp.where(pos_row == row32.astype(F32), 1.0, 0.0).astype(BF16)
    from_sorted = jnp.where(pos_col == col32.astype(F32), 1.0, 0.0).astype(BF16)
    whole_pos = patch_col * float(ROWS) + rank_col + (i * 8).astype(F32)
    row128 = lax.broadcasted_iota(jnp.int32, (32, 128), 0)
    lane128 = lax.broadcasted_iota(jnp.int32, (32, 128), 1)
    placed = jnp.where(lane128 == row128 + (i % 4) * 32, whole_pos, 0.0)
    pos_buf[i] = jnp.broadcast_to(jnp.sum(placed, axis=0, keepdims=True), (8, 128))

    loads[0].wait()
    lax.fori_loop(0, SEQ, start_w, 0)

    @pl.when(is_first)
    def _():
        sorted_rows[...] = jnp.dot(to_sorted, hid[...], preferred_element_type=F32)
        for m in range(MICRO):
            for k in range(CHUNKS):
                pieces = [
                    sorted_rows[8 * m : 8 * m + 8, COLS * j + CW * k : COLS * j + CW * (k + 1)] for j in range(SEQ)
                ]
                x_buf[MICRO + m, 0, k, 0] = jnp.concatenate(pieces, axis=0).astype(BF16)

    is_own_out = jnp.logical_and(is_last, i == out_col)
    expected = (
        (SEQ - 1)
        + jnp.where(is_last, SEQ, N_DIRECT)
        - jnp.where(is_own_out, 1, 0)
    )
    pl.semaphore_wait(barrier, expected)

    def pos_copy(k):
        return pltpu.make_async_remote_copy(
            src_ref=pos_buf.at[i], dst_ref=pos_buf.at[i], send_sem=pos_send.at[k], recv_sem=pos_recv.at[i],
            device_id=(c, s, (i + k) % SEQ), device_id_type=MESH,
        )

    def pos_arrival(b):
        return pltpu.make_async_remote_copy(
            src_ref=pos_buf.at[b], dst_ref=pos_buf.at[b], send_sem=pos_send.at[0], recv_sem=pos_recv.at[b],
            device_id=(c, s, sib), device_id_type=MESH,
        )

    def slot_of(m):
        return m + jnp.where(is_first, MICRO, 0)

    def remote(src, dst, send, recv, target):
        return pltpu.make_async_remote_copy(
            src_ref=src, dst_ref=dst, send_sem=send, recv_sem=recv, device_id=target, device_id_type=MESH
        )

    def region(m, side, k, group):
        low, high = GROUPS[group]
        return x_buf.at[slot_of(m), side, k, pl.ds(low, high - low)]

    def plane_copy(m, k, n):
        slot = slot_of(m)
        group = DIRECT if n < N_DIRECT else RELAY
        return remote(
            x_buf.at[slot, 0, k, 0], x_buf.at[slot, 0, k, BACK[n]],
            plane_sem.at[m], recv_sem.at[m, 0, group, k], (c, s, at(n, relay_flip)),
        )

    def fwd_copy(m, k, group):
        return remote(
            region(m, 0, k, group), region(m, 1, k, group), fwd_sem.at[m], recv_sem.at[m, 1, group, k], (c, s, sib)
        )

    def next_copy(m, k, n):
        return remote(
            x_out.at[m, k], x_buf.at[m, 0, k, BACK[n]],
            next_sem.at[m], recv_sem.at[m, 0, OWN if n == 0 else DIRECT, k], (c, s + 1, at(n)),
        )

    def arrive(m, side, k, group):
        here = region(m, side, k, group)
        remote(here, here, fwd_sem.at[m], recv_sem.at[m, side, group, k], (c, s, sib)).wait_recv()

    def take(m, group):
        for k in range(CHUNKS):
            arrive(m, 0, k, group)
            fwd_copy(m, k, group).start()

    def take_sib(m, *groups):
        for group in groups:
            for k in range(CHUNKS):
                arrive(m, 1, k, group)

    def spread(m):
        for k in range(CHUNKS):
            @pl.when(s > 0)
            def _():
                arrive(m, 0, k, OWN)

            for n in range(*GROUPS[RELAY]):
                plane_copy(m, k, n).start()
            fwd_copy(m, k, OWN).start()

    def spread_first(m):
        @pl.when(is_first)
        def _():
            for k in range(CHUNKS):
                for n in range(*GROUPS[DIRECT]):
                    plane_copy(m, k, n).start()
            spread(m)

    spread_first(0)

    def send_pos(k, carry):
        pos_copy(k).start()
        return carry

    lax.fori_loop(1, SEQ, send_pos, 0)

    loads[1].wait()
    colsum[...] = jnp.zeros_like(colsum)
    shifted[...] = jnp.zeros_like(shifted)

    def fold(b, carry):
        w_copy(b).wait()
        gain = jnp.concatenate(
            [jnp.broadcast_to(1.0 + mod[pl.ds(32 + 2 * b + n, 1), :], (128, 128)).T for n in range(2)], axis=0
        )
        gain = jnp.concatenate([gain, gain], axis=1)
        shift = jnp.broadcast_to(
            jnp.concatenate([mod[pl.ds(2 * b + n, 1), :] for n in range(2)], axis=1), (8, COLS)
        )
        shift_high = shift.astype(BF16)
        shift_low = (shift - shift_high.astype(F32)).astype(BF16)
        shift_both = jnp.concatenate([shift_high, shift_low], axis=0)
        ones = jnp.ones((8, COLS), BF16)
        for t in range(3):
            raw = w_buf[b, t]
            shifted[t] += jnp.dot(shift_both, raw, preferred_element_type=F32)
            scaled = (raw.astype(F32) * gain).astype(BF16)
            w_buf[b, t] = scaled
            colsum[t] += jnp.dot(ones, scaled, preferred_element_type=F32)
        return carry

    lax.fori_loop(0, SEQ // 2, fold, 0)

    spread_first(1)

    lax.fori_loop(SEQ // 2, SEQ, fold, 0)

    spread_first(2)

    loads[2].wait()

    def wait_pos(k, carry):
        pos_arrival((i + k) % SEQ).wait_recv()
        return carry

    lax.fori_loop(1, SEQ, wait_pos, 0)
    pos_all = jnp.concatenate(
        [sum(pos_buf[4 * g + n, 0:1, :] for n in range(4)) for g in range(4)], axis=1
    )
    for g in range(4):
        rows = lax.broadcasted_iota(jnp.int32, (128, 512), 0).astype(F32) + float(128 * g)
        pick = jnp.where(pos_all == rows, 1.0, 0.0).astype(BF16)
        for t in range(2):
            kv[t, 128 * g : 128 * g + 128, :] = jnp.dot(
                pick, stale[t], preferred_element_type=F32
            ).astype(BF16)

    spread_first(3)

    @pl.when(s > 0)
    def _():
        spread(0)

    def block(m, side, n):
        return jnp.concatenate([x_buf[m, side, k, n] for k in range(CHUNKS)], axis=1)

    def project(m, side, low, high):
        parts = [block(m, side, n) for n in range(low, high)]
        rows = [source(side, n) for n in range(low, high)]
        fresh = side == 0 and low == 0
        for t in range(3):
            total = sum(jnp.dot(part, w_buf[b, t], preferred_element_type=F32) for part, b in zip(parts, rows))
            acc[t] = total if fresh else acc[t] + total
        one = jnp.zeros((ROWS, 128), F32) if fresh else sum1[...]
        two = jnp.zeros((ROWS, 128), F32) if fresh else sum2[...]
        for part in parts:
            wide = part.astype(F32)
            square = wide * wide
            one = one + wide[:, :128] + wide[:, 128:]
            two = two + square[:, :128] + square[:, 128:]
        sum1[...] = one
        sum2[...] = two

    scaling = 1.0 / (HD ** 0.5)

    def patch_step(m, carry):
        @pl.when(is_first)
        def _():
            take(m, DIRECT)
            take(m, RELAY)
            take_sib(m, OWN, DIRECT, RELAY)

            def where_is(b):
                chip = 0
                for n in range(1, CHIPS):
                    chip = chip + jnp.where(at(n) // 2 == b // 2, n, 0)
                return (b + core) % 2, chip

            homes = [where_is(b) for b in range(SEQ)]
            for n in range(CHIPS):
                span = pl.ds(pl.multiple_of((at(n) // 2) * 16, 16), 16)
                for k in range(CHUNKS):
                    pieces = [x_buf[MICRO + m, side, k, chip, span, :].astype(F32) for side, chip in homes]
                    for half in range(2):
                        x_buf[m, (half + core) % 2, k, n] = jnp.concatenate(
                            [piece[8 * half : 8 * half + 8] for piece in pieces], axis=0
                        ).astype(BF16)

        @pl.when(s > 0)
        def _():
            take(m, DIRECT)

        project(m, 0, 0, N_DIRECT)

        @pl.when(s > 0)
        def _():
            @pl.when(m < MICRO - 1)
            def _():
                spread(m + 1)

            take(m, RELAY)
            take_sib(m, OWN, DIRECT)

        project(m, 1, 0, N_DIRECT)
        project(m, 0, N_DIRECT, CHIPS)

        @pl.when(s > 0)
        def _():
            take_sib(m, RELAY)

        project(m, 1, N_DIRECT, CHIPS)

        mean = jnp.sum(sum1[...], axis=1, keepdims=True) * (1.0 / D)
        var = jnp.sum(sum2[...], axis=1, keepdims=True) * (1.0 / D) - mean * mean
        inv = lax.rsqrt(var + NORM_EPS)

        def finish(t):
            bias = shifted[t, 0:1] + shifted[t, 8:9]
            return (inv * (acc[t] - mean * colsum[t, 0:1]) + bias).astype(BF16)

        query = finish(0)
        rows = pl.ds(pl.multiple_of(m * ROWS, ROWS), ROWS)
        kv[0, rows, :] = finish(1)
        kv[1, rows, :] = finish(2)
        old = block(m, 0, 0)
        for h in range(2):
            cols = slice(h * HD, (h + 1) * HD)
            scores = lax.dot_general(
                query[:, cols], kv[0, :, cols], (((1,), (1,)), ((), ())), preferred_element_type=F32
            )
            top = jnp.max(scores, axis=1, keepdims=True)
            weights = jnp.exp((scores - top) * scaling)
            norm = jnp.sum(weights, axis=1, keepdims=True)
            mixed = jnp.dot(weights.astype(BF16), kv[1, :, cols], preferred_element_type=F32) / norm
            mixed = mixed.astype(BF16).astype(F32)
            fresh = (old[:, cols].astype(F32) + mod[pl.ds(64 + 2 * i + h, 1), :] * mixed).astype(BF16)
            x_out[m, h] = fresh

            @pl.when(s < PIPE - 1)
            def _():
                next_copy(m, h, 0).start()
                if h == 1:
                    for k in range(CHUNKS):
                        for n in range(1, N_DIRECT):
                            next_copy(m, k, n).start()

        @pl.when(is_last)
        def _():
            done = jnp.concatenate([x_out[m, k] for k in range(CHUNKS)], axis=1).astype(F32)
            for b in range(SEQ):
                piece = done[8 * b : 8 * b + 8]
                fin_out[m, b] = jnp.concatenate([piece[:, :128], piece[:, 128:]], axis=0).astype(BF16)

            @pl.when(is_own_out)
            def _():
                home_copy(m).start()

                def send(k, inner):
                    fin_copy(m, (i + k) % SEQ).start()
                    return inner

                lax.fori_loop(1, SEQ, send, 0)

            @pl.when(jnp.logical_not(is_own_out))
            def _():
                for b in range(SEQ):
                    fin_copy(m, b).start()

        return carry

    def fin_copy(m, b):
        return remote(
            fin_out.at[m, b], fin_in.at[c, m], fin_send.at[m], fin_recv.at[c, m], (i // PIPE, i % PIPE, b)
        )

    def home_copy(m):
        return pltpu.make_async_copy(fin_out.at[m, i], fin_in.at[c, m], fin_recv.at[c, m])

    lax.fori_loop(0, MICRO, patch_step, 0)

    def left(ref, sem):
        remote(ref, ref, sem, recv_sem.at[0, 0, 0, 0], (c, s, sib)).wait_send()

    def drain_pos(k, carry):
        pos_copy(k).wait_send()
        return carry

    lax.fori_loop(1, SEQ, drain_pos, 0)

    for m in range(MICRO):
        left(x_buf.at[0, 0], fwd_sem.at[m])


        @pl.when(is_first)
        def _():
            left(x_buf.at[0, 0, :, pl.ds(0, CHIPS - 1)], plane_sem.at[m])

        @pl.when(s > 0)
        def _():
            left(x_buf.at[0, 0, :, pl.ds(0, CHIPS - N_DIRECT)], plane_sem.at[m])

        @pl.when(s < PIPE - 1)
        def _():
            left(x_buf.at[0, 0, :, pl.ds(0, N_DIRECT)], next_sem.at[m])

        @pl.when(jnp.logical_and(is_last, is_own_out))
        def _():
            left(fin_out.at[m, pl.ds(0, SEQ - 1)], fin_send.at[m])

        @pl.when(jnp.logical_and(is_last, jnp.logical_not(is_own_out)))
        def _():
            left(fin_out.at[m], fin_send.at[m])

    guided = []
    for m in range(MICRO):
        for branch in range(2):
            here = fin_in.at[branch, m]
            remote(here, here, fin_send.at[m], fin_recv.at[branch, m], (c, s, sib)).wait_recv()
        cond = fin_in[0, m].astype(F32)
        uncond = fin_in[1, m].astype(F32)
        piece = uncond + GUIDANCE * (cond - uncond)
        guided.append(jnp.concatenate([piece[:8], piece[8:]], axis=1))
    guided = jnp.concatenate(guided, axis=0).astype(BF16)
    out_ref[...] = jnp.dot(from_sorted, guided, preferred_element_type=F32).astype(BF16)


def body(hidden, modulation, qkv_weight, stale_cache, patch_of):
    vmem, dma = pltpu.VMEM, pltpu.SemaphoreType.DMA
    hbm = pl.BlockSpec(memory_space=pl.ANY)
    return pl.pallas_call(
        kernel,
        out_shape=jax.ShapeDtypeStruct((32, COLS), BF16),
        in_specs=[hbm, hbm, hbm, hbm, pl.BlockSpec(memory_space=pltpu.VMEM)],
        out_specs=pl.BlockSpec(memory_space=pltpu.VMEM),
        scratch_shapes=[
            vmem((2 * MICRO, 2, CHUNKS, CHIPS, ROWS, CW), BF16),
            vmem((SEQ, 3, COLS, COLS), BF16),
            vmem((32, D), BF16),
            vmem((96, 128), F32),
            vmem((2, 512, COLS), BF16),
            vmem((32, D), F32),
            vmem((2, 512, COLS), BF16),
            vmem((3, ROWS, COLS), F32),
            vmem((ROWS, 128), F32),
            vmem((ROWS, 128), F32),
            vmem((3, 8, COLS), F32),
            vmem((3, 16, COLS), F32),
            vmem((SEQ, 8, 128), F32),
            vmem((MICRO, CHUNKS, ROWS, CW), BF16),
            vmem((MICRO, SEQ, 16, 128), BF16),
            vmem((2, MICRO, 16, 128), BF16),
            dma((3,)),
            dma((SEQ,)),
            dma((SEQ,)),
            dma((SEQ,)),
            dma((MICRO,)),
            dma((MICRO,)),
            dma((MICRO,)),
            dma((MICRO, 2, 3, CHUNKS)),
            dma((MICRO,)),
            dma((2, MICRO)),
        ],
        compiler_params=pltpu.CompilerParams(
            collective_id=0, has_side_effects=True, vmem_limit_bytes=56 * 2**20
        ),
        cost_estimate=pl.CostEstimate(flops=4 * 10**9, bytes_accessed=8 * 2**20, transcendentals=10**6),
        name="layers",
    )(hidden, modulation.reshape(96, 128), qkv_weight, stale_cache, patch_of.reshape(1, 32))


def solution(mesh):
    placed = (
        P("cfg", "seq", None),
        P("pipe", None, None),
        P("pipe", None, None, "seq"),
        P("cfg", "pipe", None, None, "seq"),
        P("seq"),
    )
    return jax.shard_map(
        body, mesh=mesh, in_specs=placed, out_specs=P("seq", ("cfg", "pipe")), check_vma=False
    )
```

```python
import functools

import jax
import jax.numpy as jnp
from jax import lax
from jax.experimental import pallas as pl
from jax.experimental.pallas import tpu as pltpu
from jax.sharding import PartitionSpec as P

F32 = jnp.float32
BF16 = jnp.bfloat16
MESH = pl.DeviceIdType.MESH

HD = 128
D = 4096
MICRO = 4
ROWS = 128
COLS = 256
SEQ = 16
PIPE = 8
GUIDANCE = 5.0
NORM_EPS = 1e-06
LOG2_E = 1.4426950408889634

OFFSETS = ((0, 0), (1, 1), (3, 1), (2, 1), (1, 0), (3, 0), (2, 0), (0, 1))
BACK = tuple(OFFSETS.index(((4 - dx) % 4, dy)) for dx, dy in OFFSETS)
CHIPS = 8
N_DIRECT = 4
GROUPS = ((0, 1), (1, N_DIRECT), (N_DIRECT, CHIPS))
OWN, DIRECT, RELAY = 0, 1, 2
CHUNKS = 2
CW = COLS // CHUNKS


def kernel(
    hid_hbm, mod_hbm, w_hbm, stale_hbm, patch_ref, out_ref,
    x_buf, w_buf, hid, mod, stale, sorted_rows, kv, acc, sum1, sum2, colsum, shifted,
    pos_buf, x_out, fin_out, fin_in,
    load_sem, w_sem, pos_send, pos_recv, plane_sem, fwd_sem, next_sem, recv_sem, fin_send, fin_recv,
):
    c = lax.axis_index("cfg")
    s = lax.axis_index("pipe")
    i = lax.axis_index("seq")
    core = i % 2
    y = (i // 2) % 2
    x = i // 4
    is_first = s == 0
    is_last = s == PIPE - 1
    relay_flip = jnp.where(is_first, 0, 1)

    def at(n, other=0):
        dx, dy = OFFSETS[n]
        return (((x + dx) % 4) * 2 + (y + dy) % 2) * 2 + (core + other) % 2

    def source(side, n):
        return at(n, side + relay_flip if n >= N_DIRECT else side)

    sib = at(0, 1)
    out_col = c * PIPE + s

    loads = [
        pltpu.make_async_copy(hid_hbm.at[0], hid, load_sem.at[0]),
        pltpu.make_async_copy(mod_hbm, mod, load_sem.at[1]),
        pltpu.make_async_copy(stale_hbm.at[0, 0], stale, load_sem.at[2]),
    ]

    def w_copy(b):
        return pltpu.make_async_copy(
            w_hbm.at[0, :, pl.ds(pl.multiple_of(b * COLS, COLS), COLS), :], w_buf.at[b], w_sem.at[b]
        )

    barrier = pltpu.get_barrier_semaphore()

    def greet(target):
        pl.semaphore_signal(barrier, inc=1, device_id=target, device_id_type=MESH)

    def greet_plane(k, carry):
        greet((c, s, (i + k) % SEQ))
        return carry

    lax.fori_loop(1, SEQ, greet_plane, 0)

    @pl.when(s > 0)
    def _():
        for n in range(N_DIRECT):
            greet((c, s - 1, at(n)))

    for branch in range(2):
        is_self = jnp.logical_and(jnp.logical_and(c == branch, is_last), i == out_col)

        @pl.when(jnp.logical_not(is_self))
        def _():
            greet((branch, PIPE - 1, out_col))

    for load in loads:
        load.start()

    def start_w(b, carry):
        w_copy(b).start()
        return carry

    patch_row = jnp.broadcast_to(patch_ref[...].astype(F32), (32, 32))
    row32 = lax.broadcasted_iota(jnp.int32, (32, 32), 0)
    col32 = lax.broadcasted_iota(jnp.int32, (32, 32), 1)
    patch_col = jnp.sum(jnp.where(row32 == col32, patch_row, 0.0), axis=1, keepdims=True)
    same = jnp.where(patch_row == patch_col, 1.0, 0.0)
    rank_col = jnp.sum(jnp.where(col32 < row32, same, 0.0), axis=1, keepdims=True)
    rank_row = jnp.sum(jnp.where(row32 < col32, same, 0.0), axis=0, keepdims=True)
    pos_row = patch_row[0:1] * 8.0 + rank_row
    pos_col = patch_col * 8.0 + rank_col
    to_sorted = jnp.where(pos_row == row32.astype(F32), 1.0, 0.0).astype(BF16)
    from_sorted = jnp.where(pos_col == col32.astype(F32), 1.0, 0.0).astype(BF16)
    whole_pos = patch_col * float(ROWS) + rank_col + (i * 8).astype(F32)
    row128 = lax.broadcasted_iota(jnp.int32, (32, 128), 0)
    lane128 = lax.broadcasted_iota(jnp.int32, (32, 128), 1)
    placed = jnp.where(lane128 == row128 + (i % 4) * 32, whole_pos, 0.0)
    pos_buf[i] = jnp.broadcast_to(jnp.sum(placed, axis=0, keepdims=True), (8, 128))

    loads[0].wait()
    lax.fori_loop(0, SEQ, start_w, 0)

    @pl.when(is_first)
    def _():
        sorted_rows[...] = jnp.dot(to_sorted, hid[...], preferred_element_type=F32)
        for m in range(MICRO):
            for k in range(CHUNKS):
                pieces = [
                    sorted_rows[8 * m : 8 * m + 8, COLS * j + CW * k : COLS * j + CW * (k + 1)] for j in range(SEQ)
                ]
                x_buf[MICRO + m, 0, k, 0] = jnp.concatenate(pieces, axis=0).astype(BF16)

    is_own_out = jnp.logical_and(is_last, i == out_col)
    expected = (
        (SEQ - 1)
        + jnp.where(is_last, SEQ, N_DIRECT)
        - jnp.where(is_own_out, 1, 0)
    )
    pl.semaphore_wait(barrier, expected)

    def pos_copy(k):
        return pltpu.make_async_remote_copy(
            src_ref=pos_buf.at[i], dst_ref=pos_buf.at[i], send_sem=pos_send.at[k], recv_sem=pos_recv.at[i],
            device_id=(c, s, (i + k) % SEQ), device_id_type=MESH,
        )

    def pos_arrival(b):
        return pltpu.make_async_remote_copy(
            src_ref=pos_buf.at[b], dst_ref=pos_buf.at[b], send_sem=pos_send.at[0], recv_sem=pos_recv.at[b],
            device_id=(c, s, sib), device_id_type=MESH,
        )

    def slot_of(m):
        return m + jnp.where(is_first, MICRO, 0)

    def remote(src, dst, send, recv, target):
        return pltpu.make_async_remote_copy(
            src_ref=src, dst_ref=dst, send_sem=send, recv_sem=recv, device_id=target, device_id_type=MESH
        )

    def region(m, side, k, group):
        low, high = GROUPS[group]
        return x_buf.at[slot_of(m), side, k, pl.ds(low, high - low)]

    def plane_copy(m, k, n):
        slot = slot_of(m)
        group = DIRECT if n < N_DIRECT else RELAY
        return remote(
            x_buf.at[slot, 0, k, 0], x_buf.at[slot, 0, k, BACK[n]],
            plane_sem.at[m], recv_sem.at[m, 0, group, k], (c, s, at(n, relay_flip)),
        )

    def fwd_copy(m, k, group):
        return remote(
            region(m, 0, k, group), region(m, 1, k, group), fwd_sem.at[m], recv_sem.at[m, 1, group, k], (c, s, sib)
        )

    def next_copy(m, k, n):
        return remote(
            x_out.at[m, k], x_buf.at[m, 0, k, BACK[n]],
            next_sem.at[m], recv_sem.at[m, 0, OWN if n == 0 else DIRECT, k], (c, s + 1, at(n)),
        )

    def arrive(m, side, k, group):
        here = region(m, side, k, group)
        remote(here, here, fwd_sem.at[m], recv_sem.at[m, side, group, k], (c, s, sib)).wait_recv()

    def take(m, group):
        for k in range(CHUNKS):
            arrive(m, 0, k, group)
            fwd_copy(m, k, group).start()

    def take_sib(m, *groups):
        for group in groups:
            for k in range(CHUNKS):
                arrive(m, 1, k, group)

    def spread(m):
        for k in range(CHUNKS):
            @pl.when(s > 0)
            def _():
                arrive(m, 0, k, OWN)

            for n in range(*GROUPS[RELAY]):
                plane_copy(m, k, n).start()
            fwd_copy(m, k, OWN).start()

    def spread_first(m):
        @pl.when(is_first)
        def _():
            for k in range(CHUNKS):
                for n in range(*GROUPS[DIRECT]):
                    plane_copy(m, k, n).start()
            spread(m)

    spread_first(0)

    def send_pos(k, carry):
        pos_copy(k).start()
        return carry

    lax.fori_loop(1, SEQ, send_pos, 0)

    loads[1].wait()
    colsum[...] = jnp.zeros_like(colsum)
    shifted[...] = jnp.zeros_like(shifted)

    def fold(b, carry):
        w_copy(b).wait()
        gain = jnp.concatenate(
            [jnp.broadcast_to(1.0 + mod[pl.ds(32 + 2 * b + n, 1), :], (128, 128)).T for n in range(2)], axis=0
        )
        gain = jnp.concatenate([gain, gain], axis=1)
        shift = jnp.broadcast_to(
            jnp.concatenate([mod[pl.ds(2 * b + n, 1), :] for n in range(2)], axis=1), (8, COLS)
        )
        shift_high = shift.astype(BF16)
        shift_low = (shift - shift_high.astype(F32)).astype(BF16)
        shift_both = jnp.concatenate([shift_high, shift_low], axis=0)
        ones = jnp.ones((8, COLS), BF16)
        for t in range(3):
            raw = w_buf[b, t]
            shifted[t] += jnp.dot(shift_both, raw, preferred_element_type=F32)
            scaled = (raw.astype(F32) * gain).astype(BF16)
            w_buf[b, t] = scaled
            colsum[t] += jnp.dot(ones, scaled, preferred_element_type=F32)
        return carry

    lax.fori_loop(0, SEQ // 2, fold, 0)

    spread_first(1)

    lax.fori_loop(SEQ // 2, SEQ, fold, 0)

    spread_first(2)

    loads[2].wait()

    def wait_pos(k, carry):
        pos_arrival((i + k) % SEQ).wait_recv()
        return carry

    lax.fori_loop(1, SEQ, wait_pos, 0)
    pos_all = jnp.concatenate(
        [sum(pos_buf[4 * g + n, 0:1, :] for n in range(4)) for g in range(4)], axis=1
    )
    for g in range(4):
        rows = lax.broadcasted_iota(jnp.int32, (128, 512), 0).astype(F32) + float(128 * g)
        pick = jnp.where(pos_all == rows, 1.0, 0.0).astype(BF16)
        for t in range(2):
            kv[t, 128 * g : 128 * g + 128, :] = jnp.dot(
                pick, stale[t], preferred_element_type=F32
            ).astype(BF16)

    spread_first(3)

    @pl.when(s > 0)
    def _():
        spread(0)

    def block(m, side, n):
        return jnp.concatenate([x_buf[m, side, k, n] for k in range(CHUNKS)], axis=1)

    def project(m, side, low, high):
        parts = [block(m, side, n) for n in range(low, high)]
        rows = [source(side, n) for n in range(low, high)]
        fresh = side == 0 and low == 0
        for t in range(3):
            total = sum(jnp.dot(part, w_buf[b, t], preferred_element_type=F32) for part, b in zip(parts, rows))
            acc[t] = total if fresh else acc[t] + total
        one = jnp.zeros((ROWS, 128), F32) if fresh else sum1[...]
        two = jnp.zeros((ROWS, 128), F32) if fresh else sum2[...]
        for part in parts:
            wide = part.astype(F32)
            square = wide * wide
            one = one + wide[:, :128] + wide[:, 128:]
            two = two + square[:, :128] + square[:, 128:]
        sum1[...] = one
        sum2[...] = two

    def project_half(m, side, k, low, high):
        pairs = [(n, n + 1) for n in range(low, high, 2)]
        parts = [jnp.concatenate([x_buf[m, side, k, n] for n in pair], axis=1) for pair in pairs]
        rows = slice(CW * k, CW * (k + 1))
        for t in range(3):
            total = acc[t]
            for part, pair in zip(parts, pairs):
                weight = jnp.concatenate([w_buf[source(side, n), t, rows, :] for n in pair], axis=0)
                total = total + jnp.dot(part, weight, preferred_element_type=F32)
            acc[t] = total
        one = sum1[...]
        two = sum2[...]
        for part in parts:
            wide = part.astype(F32)
            square = wide * wide
            one = one + wide[:, :128] + wide[:, 128:]
            two = two + square[:, :128] + square[:, 128:]
        sum1[...] = one
        sum2[...] = two

    scaling = LOG2_E / (HD ** 0.5)

    def patch_step(m, carry):
        @pl.when(is_first)
        def _():
            take(m, DIRECT)
            take(m, RELAY)
            take_sib(m, OWN, DIRECT, RELAY)

            def where_is(b):
                chip = 0
                for n in range(1, CHIPS):
                    chip = chip + jnp.where(at(n) // 2 == b // 2, n, 0)
                return (b + core) % 2, chip

            homes = [where_is(b) for b in range(SEQ)]
            for n in range(CHIPS):
                span = pl.ds(pl.multiple_of((at(n) // 2) * 16, 16), 16)
                for k in range(CHUNKS):
                    pieces = [x_buf[MICRO + m, side, k, chip, span, :].astype(F32) for side, chip in homes]
                    for half in range(2):
                        x_buf[m, (half + core) % 2, k, n] = jnp.concatenate(
                            [piece[8 * half : 8 * half + 8] for piece in pieces], axis=0
                        ).astype(BF16)

        @pl.when(s > 0)
        def _():
            take(m, DIRECT)

        @pl.when(s > 0)
        def _():
            @pl.when(m < MICRO - 1)
            def _():
                spread(m + 1)

        project(m, 0, 0, N_DIRECT)

        @pl.when(s > 0)
        def _():

            take(m, RELAY)
            take_sib(m, OWN, DIRECT)

        project(m, 1, 0, N_DIRECT)
        project(m, 0, N_DIRECT, CHIPS)

        for k in range(CHUNKS):
            @pl.when(s > 0)
            def _():
                arrive(m, 1, k, RELAY)

            project_half(m, 1, k, N_DIRECT, CHIPS)

        mean = jnp.sum(sum1[...], axis=1, keepdims=True) * (1.0 / D)
        var = jnp.sum(sum2[...], axis=1, keepdims=True) * (1.0 / D) - mean * mean
        inv = lax.rsqrt(var + NORM_EPS)

        def finish(t):
            bias = shifted[t, 0:1] + shifted[t, 8:9]
            return (inv * (acc[t] - mean * colsum[t, 0:1]) + bias).astype(BF16)

        query = finish(0)
        rows = pl.ds(pl.multiple_of(m * ROWS, ROWS), ROWS)
        kv[0, rows, :] = finish(1)
        kv[1, rows, :] = finish(2)
        old = block(m, 0, 0)
        for h in range(2):
            cols = slice(h * HD, (h + 1) * HD)
            scores = lax.dot_general(
                query[:, cols], kv[0, :, cols], (((1,), (1,)), ((), ())), preferred_element_type=F32
            )
            top = jnp.max(scores, axis=1, keepdims=True)
            weights = jnp.exp2((scores - top) * scaling)
            norm = 1.0 / jnp.sum(weights, axis=1, keepdims=True)
            mixed = jnp.dot(weights.astype(BF16), kv[1, :, cols], preferred_element_type=F32) * norm
            mixed = mixed.astype(BF16).astype(F32)
            fresh = (old[:, cols].astype(F32) + mod[pl.ds(64 + 2 * i + h, 1), :] * mixed).astype(BF16)
            x_out[m, h] = fresh

            @pl.when(s < PIPE - 1)
            def _():
                next_copy(m, h, 0).start()
                if h == 1:
                    for k in range(CHUNKS):
                        for n in range(1, N_DIRECT):
                            next_copy(m, k, n).start()

        @pl.when(is_last)
        def _():
            done = jnp.concatenate([x_out[m, k] for k in range(CHUNKS)], axis=1).astype(F32)
            for b in range(SEQ):
                piece = done[8 * b : 8 * b + 8]
                fin_out[m, b] = jnp.concatenate([piece[:, :128], piece[:, 128:]], axis=0).astype(BF16)

            @pl.when(is_own_out)
            def _():
                home_copy(m).start()

                def send(k, inner):
                    fin_copy(m, (i + k) % SEQ).start()
                    return inner

                lax.fori_loop(1, SEQ, send, 0)

            @pl.when(jnp.logical_not(is_own_out))
            def _():
                for b in range(SEQ):
                    fin_copy(m, b).start()

        return carry

    def fin_copy(m, b):
        return remote(
            fin_out.at[m, b], fin_in.at[c, m], fin_send.at[m], fin_recv.at[c, m], (i // PIPE, i % PIPE, b)
        )

    def home_copy(m):
        return pltpu.make_async_copy(fin_out.at[m, i], fin_in.at[c, m], fin_recv.at[c, m])

    lax.fori_loop(0, MICRO, patch_step, 0)

    def left(ref, sem):
        remote(ref, ref, sem, recv_sem.at[0, 0, 0, 0], (c, s, sib)).wait_send()

    def drain_pos(k, carry):
        pos_copy(k).wait_send()
        return carry

    lax.fori_loop(1, SEQ, drain_pos, 0)

    for m in range(MICRO):
        left(x_buf.at[0, 0], fwd_sem.at[m])


        @pl.when(is_first)
        def _():
            left(x_buf.at[0, 0, :, pl.ds(0, CHIPS - 1)], plane_sem.at[m])

        @pl.when(s > 0)
        def _():
            left(x_buf.at[0, 0, :, pl.ds(0, CHIPS - N_DIRECT)], plane_sem.at[m])

        @pl.when(s < PIPE - 1)
        def _():
            left(x_buf.at[0, 0, :, pl.ds(0, N_DIRECT)], next_sem.at[m])

        @pl.when(jnp.logical_and(is_last, is_own_out))
        def _():
            left(fin_out.at[m, pl.ds(0, SEQ - 1)], fin_send.at[m])

        @pl.when(jnp.logical_and(is_last, jnp.logical_not(is_own_out)))
        def _():
            left(fin_out.at[m], fin_send.at[m])

    guided = []
    for m in range(MICRO):
        for branch in range(2):
            here = fin_in.at[branch, m]
            remote(here, here, fin_send.at[m], fin_recv.at[branch, m], (c, s, sib)).wait_recv()
        cond = fin_in[0, m].astype(F32)
        uncond = fin_in[1, m].astype(F32)
        piece = uncond + GUIDANCE * (cond - uncond)
        guided.append(jnp.concatenate([piece[:8], piece[8:]], axis=1))
    guided = jnp.concatenate(guided, axis=0).astype(BF16)
    out_ref[...] = jnp.dot(from_sorted, guided, preferred_element_type=F32).astype(BF16)


def body(hidden, modulation, qkv_weight, stale_cache, patch_of):
    vmem, dma = pltpu.VMEM, pltpu.SemaphoreType.DMA
    hbm = pl.BlockSpec(memory_space=pl.ANY)
    return pl.pallas_call(
        kernel,
        out_shape=jax.ShapeDtypeStruct((32, COLS), BF16),
        in_specs=[hbm, hbm, hbm, hbm, pl.BlockSpec(memory_space=pltpu.VMEM)],
        out_specs=pl.BlockSpec(memory_space=pltpu.VMEM),
        scratch_shapes=[
            vmem((2 * MICRO, 2, CHUNKS, CHIPS, ROWS, CW), BF16),
            vmem((SEQ, 3, COLS, COLS), BF16),
            vmem((32, D), BF16),
            vmem((96, 128), F32),
            vmem((2, 512, COLS), BF16),
            vmem((32, D), F32),
            vmem((2, 512, COLS), BF16),
            vmem((3, ROWS, COLS), F32),
            vmem((ROWS, 128), F32),
            vmem((ROWS, 128), F32),
            vmem((3, 8, COLS), F32),
            vmem((3, 16, COLS), F32),
            vmem((SEQ, 8, 128), F32),
            vmem((MICRO, CHUNKS, ROWS, CW), BF16),
            vmem((MICRO, SEQ, 16, 128), BF16),
            vmem((2, MICRO, 16, 128), BF16),
            dma((3,)),
            dma((SEQ,)),
            dma((SEQ,)),
            dma((SEQ,)),
            dma((MICRO,)),
            dma((MICRO,)),
            dma((MICRO,)),
            dma((MICRO, 2, 3, CHUNKS)),
            dma((MICRO,)),
            dma((2, MICRO)),
        ],
        compiler_params=pltpu.CompilerParams(
            collective_id=0, has_side_effects=True, vmem_limit_bytes=56 * 2**20
        ),
        cost_estimate=pl.CostEstimate(flops=4 * 10**9, bytes_accessed=8 * 2**20, transcendentals=10**6),
        name="layers",
    )(hidden, modulation.reshape(96, 128), qkv_weight, stale_cache, patch_of.reshape(1, 32))


def solution(mesh):
    placed = (
        P("cfg", "seq", None),
        P("pipe", None, None),
        P("pipe", None, None, "seq"),
        P("cfg", "pipe", None, None, "seq"),
        P("seq"),
    )
    return jax.shard_map(
        body, mesh=mesh, in_specs=placed, out_specs=P("seq", ("cfg", "pipe")), check_vma=False
    )
```

```python
import functools

import jax
import jax.numpy as jnp
from jax import lax
from jax.experimental import pallas as pl
from jax.experimental.pallas import tpu as pltpu
from jax.sharding import PartitionSpec as P

F32 = jnp.float32
BF16 = jnp.bfloat16
MESH = pl.DeviceIdType.MESH

HD = 128
D = 4096
MICRO = 4
ROWS = 128
COLS = 256
SEQ = 16
PIPE = 8
GUIDANCE = 5.0
NORM_EPS = 1e-06
LOG2_E = 1.4426950408889634

OFFSETS = ((0, 0), (1, 1), (3, 1), (2, 1), (0, 1), (1, 0), (3, 0), (2, 0))
BACK = tuple(OFFSETS.index(((4 - dx) % 4, dy)) for dx, dy in OFFSETS)
CHIPS = 8
N_DIRECT = 4
GROUPS = ((0, 1), (1, N_DIRECT), (N_DIRECT, CHIPS - 1), (CHIPS - 1, CHIPS))
OWN, DIRECT, RELAY, FAR = 0, 1, 2, 3
RELAY_ORDER = (5, 6, 7, 4)
CHUNKS = 2
CW = COLS // CHUNKS


def kernel(
    hid_hbm, mod_hbm, w_hbm, stale_hbm, patch_ref, out_ref,
    x_buf, w_buf, hid, mod, stale, sorted_rows, kv, acc, sum1, sum2, colsum, shifted,
    pos_buf, x_out, fin_out, fin_in,
    load_sem, w_sem, pos_send, pos_recv, plane_sem, fwd_sem, next_sem, recv_sem, fin_send, fin_recv,
):
    c = lax.axis_index("cfg")
    s = lax.axis_index("pipe")
    i = lax.axis_index("seq")
    core = i % 2
    y = (i // 2) % 2
    x = i // 4
    is_first = s == 0
    is_last = s == PIPE - 1
    relay_flip = jnp.where(is_first, 0, 1)

    def at(n, other=0):
        dx, dy = OFFSETS[n]
        return (((x + dx) % 4) * 2 + (y + dy) % 2) * 2 + (core + other) % 2

    def source(side, n):
        return at(n, side + relay_flip if n > 0 else side)

    sib = at(0, 1)
    out_col = c * PIPE + s

    loads = [
        pltpu.make_async_copy(hid_hbm.at[0], hid, load_sem.at[0]),
        pltpu.make_async_copy(mod_hbm, mod, load_sem.at[1]),
        pltpu.make_async_copy(stale_hbm.at[0, 0], stale, load_sem.at[2]),
    ]

    def w_copy(b):
        return pltpu.make_async_copy(
            w_hbm.at[0, :, pl.ds(pl.multiple_of(b * COLS, COLS), COLS), :], w_buf.at[b], w_sem.at[b]
        )

    barrier = pltpu.get_barrier_semaphore()

    def greet(target):
        pl.semaphore_signal(barrier, inc=1, device_id=target, device_id_type=MESH)

    def greet_plane(k, carry):
        greet((c, s, (i + k) % SEQ))
        return carry

    lax.fori_loop(1, SEQ, greet_plane, 0)

    @pl.when(s > 0)
    def _():
        for n in range(N_DIRECT):
            greet((c, s - 1, at(n, 1 if n else 0)))

    for branch in range(2):
        is_self = jnp.logical_and(jnp.logical_and(c == branch, is_last), i == out_col)

        @pl.when(jnp.logical_not(is_self))
        def _():
            greet((branch, PIPE - 1, out_col))

    for load in loads:
        load.start()

    def start_w(b, carry):
        w_copy(b).start()
        return carry

    patch_row = jnp.broadcast_to(patch_ref[...].astype(F32), (32, 32))
    row32 = lax.broadcasted_iota(jnp.int32, (32, 32), 0)
    col32 = lax.broadcasted_iota(jnp.int32, (32, 32), 1)
    patch_col = jnp.sum(jnp.where(row32 == col32, patch_row, 0.0), axis=1, keepdims=True)
    same = jnp.where(patch_row == patch_col, 1.0, 0.0)
    rank_col = jnp.sum(jnp.where(col32 < row32, same, 0.0), axis=1, keepdims=True)
    rank_row = jnp.sum(jnp.where(row32 < col32, same, 0.0), axis=0, keepdims=True)
    pos_row = patch_row[0:1] * 8.0 + rank_row
    pos_col = patch_col * 8.0 + rank_col
    to_sorted = jnp.where(pos_row == row32.astype(F32), 1.0, 0.0).astype(BF16)
    from_sorted = jnp.where(pos_col == col32.astype(F32), 1.0, 0.0).astype(BF16)
    whole_pos = patch_col * float(ROWS) + rank_col + (i * 8).astype(F32)
    row128 = lax.broadcasted_iota(jnp.int32, (32, 128), 0)
    lane128 = lax.broadcasted_iota(jnp.int32, (32, 128), 1)
    placed = jnp.where(lane128 == row128 + (i % 4) * 32, whole_pos, 0.0)
    pos_buf[i] = jnp.broadcast_to(jnp.sum(placed, axis=0, keepdims=True), (8, 128))

    loads[0].wait()
    lax.fori_loop(0, SEQ, start_w, 0)

    @pl.when(is_first)
    def _():
        sorted_rows[...] = jnp.dot(to_sorted, hid[...], preferred_element_type=F32)
        for m in range(MICRO):
            for k in range(CHUNKS):
                pieces = [
                    sorted_rows[8 * m : 8 * m + 8, COLS * j + CW * k : COLS * j + CW * (k + 1)] for j in range(SEQ)
                ]
                x_buf[MICRO + m, 0, k, 0] = jnp.concatenate(pieces, axis=0).astype(BF16)

    is_own_out = jnp.logical_and(is_last, i == out_col)
    expected = (
        (SEQ - 1)
        + jnp.where(is_last, SEQ, N_DIRECT)
        - jnp.where(is_own_out, 1, 0)
    )
    pl.semaphore_wait(barrier, expected)

    def pos_copy(k):
        return pltpu.make_async_remote_copy(
            src_ref=pos_buf.at[i], dst_ref=pos_buf.at[i], send_sem=pos_send.at[k], recv_sem=pos_recv.at[i],
            device_id=(c, s, (i + k) % SEQ), device_id_type=MESH,
        )

    def pos_arrival(b):
        return pltpu.make_async_remote_copy(
            src_ref=pos_buf.at[b], dst_ref=pos_buf.at[b], send_sem=pos_send.at[0], recv_sem=pos_recv.at[b],
            device_id=(c, s, sib), device_id_type=MESH,
        )

    def slot_of(m):
        return m + jnp.where(is_first, MICRO, 0)

    def remote(src, dst, send, recv, target):
        return pltpu.make_async_remote_copy(
            src_ref=src, dst_ref=dst, send_sem=send, recv_sem=recv, device_id=target, device_id_type=MESH
        )

    def region(m, side, k, group):
        low, high = GROUPS[group]
        return x_buf.at[slot_of(m), side, k, pl.ds(low, high - low)]

    def plane_copy(m, k, n):
        slot = slot_of(m)
        group = DIRECT if n < N_DIRECT else RELAY if n < CHIPS - 1 else FAR
        return remote(
            x_buf.at[slot, 0, k, 0], x_buf.at[slot, 0, k, BACK[n]],
            plane_sem.at[m], recv_sem.at[m, 0, group, k], (c, s, at(n, relay_flip)),
        )

    def fwd_copy(m, k, group):
        return remote(
            region(m, 0, k, group), region(m, 1, k, group), fwd_sem.at[m], recv_sem.at[m, 1, group, k], (c, s, sib)
        )

    def next_copy(m, k, n):
        return remote(
            x_out.at[m, k], x_buf.at[m, 0, k, BACK[n]],
            next_sem.at[m], recv_sem.at[m, 0, OWN if n == 0 else DIRECT, k], (c, s + 1, at(n, 1 if n else 0)),
        )

    def arrive(m, side, k, group):
        here = region(m, side, k, group)
        remote(here, here, fwd_sem.at[m], recv_sem.at[m, side, group, k], (c, s, sib)).wait_recv()

    def take(m, *groups):
        for k in range(CHUNKS):
            for group in groups:
                arrive(m, 0, k, group)
                fwd_copy(m, k, group).start()

    def take_sib(m, *groups):
        for group in groups:
            for k in range(CHUNKS):
                arrive(m, 1, k, group)

    def spread(m):
        for k in range(CHUNKS):
            @pl.when(s > 0)
            def _():
                arrive(m, 0, k, OWN)

            for n in RELAY_ORDER:
                plane_copy(m, k, n).start()
            fwd_copy(m, k, OWN).start()

    def spread_first(m):
        @pl.when(is_first)
        def _():
            for k in range(CHUNKS):
                for n in range(*GROUPS[DIRECT]):
                    plane_copy(m, k, n).start()
            spread(m)

    spread_first(0)

    def send_pos(k, carry):
        pos_copy(k).start()
        return carry

    lax.fori_loop(1, SEQ, send_pos, 0)

    loads[1].wait()
    colsum[...] = jnp.zeros_like(colsum)
    shifted[...] = jnp.zeros_like(shifted)

    def fold(b, carry):
        w_copy(b).wait()
        gain = jnp.concatenate(
            [jnp.broadcast_to(1.0 + mod[pl.ds(32 + 2 * b + n, 1), :], (128, 128)).T for n in range(2)], axis=0
        )
        gain = jnp.concatenate([gain, gain], axis=1)
        shift = jnp.broadcast_to(
            jnp.concatenate([mod[pl.ds(2 * b + n, 1), :] for n in range(2)], axis=1), (8, COLS)
        )
        shift_high = shift.astype(BF16)
        shift_low = (shift - shift_high.astype(F32)).astype(BF16)
        shift_both = jnp.concatenate([shift_high, shift_low], axis=0)
        ones = jnp.ones((8, COLS), BF16)
        for t in range(3):
            raw = w_buf[b, t]
            shifted[t] += jnp.dot(shift_both, raw, preferred_element_type=F32)
            scaled = (raw.astype(F32) * gain).astype(BF16)
            w_buf[b, t] = scaled
            colsum[t] += jnp.dot(ones, scaled, preferred_element_type=F32)
        return carry

    lax.fori_loop(0, SEQ // 2, fold, 0)

    spread_first(1)

    lax.fori_loop(SEQ // 2, SEQ, fold, 0)

    spread_first(2)

    loads[2].wait()

    def wait_pos(k, carry):
        pos_arrival((i + k) % SEQ).wait_recv()
        return carry

    lax.fori_loop(1, SEQ, wait_pos, 0)
    pos_all = jnp.concatenate(
        [sum(pos_buf[4 * g + n, 0:1, :] for n in range(4)) for g in range(4)], axis=1
    )
    for g in range(4):
        rows = lax.broadcasted_iota(jnp.int32, (128, 512), 0).astype(F32) + float(128 * g)
        pick = jnp.where(pos_all == rows, 1.0, 0.0).astype(BF16)
        for t in range(2):
            kv[t, 128 * g : 128 * g + 128, :] = jnp.dot(
                pick, stale[t], preferred_element_type=F32
            ).astype(BF16)

    spread_first(3)

    @pl.when(s > 0)
    def _():
        spread(0)

    def block(m, side, n):
        return jnp.concatenate([x_buf[m, side, k, n] for k in range(CHUNKS)], axis=1)

    def project(m, side, low, high):
        parts = [block(m, side, n) for n in range(low, high)]
        rows = [source(side, n) for n in range(low, high)]
        fresh = side == 0 and low == 0
        for t in range(3):
            total = sum(jnp.dot(part, w_buf[b, t], preferred_element_type=F32) for part, b in zip(parts, rows))
            acc[t] = total if fresh else acc[t] + total
        one = jnp.zeros((ROWS, 128), F32) if fresh else sum1[...]
        two = jnp.zeros((ROWS, 128), F32) if fresh else sum2[...]
        for part in parts:
            wide = part.astype(F32)
            square = wide * wide
            one = one + wide[:, :128] + wide[:, 128:]
            two = two + square[:, :128] + square[:, 128:]
        sum1[...] = one
        sum2[...] = two

    def project_half(m, side, k, low, high):
        pairs = [(n, n + 1) for n in range(low, high, 2)]
        parts = [jnp.concatenate([x_buf[m, side, k, n] for n in pair], axis=1) for pair in pairs]
        rows = slice(CW * k, CW * (k + 1))
        for t in range(3):
            total = acc[t]
            for part, pair in zip(parts, pairs):
                weight = jnp.concatenate([w_buf[source(side, n), t, rows, :] for n in pair], axis=0)
                total = total + jnp.dot(part, weight, preferred_element_type=F32)
            acc[t] = total
        one = sum1[...]
        two = sum2[...]
        for part in parts:
            wide = part.astype(F32)
            square = wide * wide
            one = one + wide[:, :128] + wide[:, 128:]
            two = two + square[:, :128] + square[:, 128:]
        sum1[...] = one
        sum2[...] = two

    scaling = LOG2_E / (HD ** 0.5)

    def patch_step(m, carry):
        @pl.when(is_first)
        def _():
            take(m, DIRECT, RELAY, FAR)
            take_sib(m, OWN, DIRECT, RELAY, FAR)

            def where_is(b):
                chip = 0
                for n in range(1, CHIPS):
                    chip = chip + jnp.where(at(n) // 2 == b // 2, n, 0)
                return (b + core) % 2, chip

            homes = [where_is(b) for b in range(SEQ)]
            for n in range(CHIPS):
                span = pl.ds(pl.multiple_of((at(n) // 2) * 16, 16), 16)
                for k in range(CHUNKS):
                    pieces = [x_buf[MICRO + m, side, k, chip, span, :].astype(F32) for side, chip in homes]
                    for half in range(2):
                        x_buf[m, (half + core) % 2, k, n] = jnp.concatenate(
                            [piece[8 * half : 8 * half + 8] for piece in pieces], axis=0
                        ).astype(BF16)

        @pl.when(s > 0)
        def _():
            @pl.when(m < MICRO - 1)
            def _():
                spread(m + 1)

            take(m, DIRECT, RELAY, FAR)

        project(m, 0, 0, N_DIRECT)
        project(m, 0, N_DIRECT, CHIPS)

        @pl.when(s > 0)
        def _():
            take_sib(m, OWN, DIRECT)

        project(m, 1, 0, N_DIRECT)

        for k in range(CHUNKS):
            @pl.when(s > 0)
            def _():
                arrive(m, 1, k, RELAY)
                arrive(m, 1, k, FAR)

            project_half(m, 1, k, N_DIRECT, CHIPS)

        mean = jnp.sum(sum1[...], axis=1, keepdims=True) * (1.0 / D)
        var = jnp.sum(sum2[...], axis=1, keepdims=True) * (1.0 / D) - mean * mean
        inv = lax.rsqrt(var + NORM_EPS)

        def finish(t):
            bias = shifted[t, 0:1] + shifted[t, 8:9]
            return (inv * (acc[t] - mean * colsum[t, 0:1]) + bias).astype(BF16)

        query = finish(0)
        rows = pl.ds(pl.multiple_of(m * ROWS, ROWS), ROWS)
        kv[0, rows, :] = finish(1)
        kv[1, rows, :] = finish(2)
        old = block(m, 0, 0)
        for h in range(2):
            cols = slice(h * HD, (h + 1) * HD)
            scores = lax.dot_general(
                query[:, cols], kv[0, :, cols], (((1,), (1,)), ((), ())), preferred_element_type=F32
            )
            top = jnp.max(scores, axis=1, keepdims=True)
            weights = jnp.exp2((scores - top) * scaling)
            norm = 1.0 / jnp.sum(weights, axis=1, keepdims=True)
            mixed = jnp.dot(weights.astype(BF16), kv[1, :, cols], preferred_element_type=F32) * norm
            mixed = mixed.astype(BF16).astype(F32)
            fresh = (old[:, cols].astype(F32) + mod[pl.ds(64 + 2 * i + h, 1), :] * mixed).astype(BF16)
            x_out[m, h] = fresh

            @pl.when(s < PIPE - 1)
            def _():
                next_copy(m, h, 0).start()
                if h == 1:
                    for k in range(CHUNKS):
                        for n in range(1, N_DIRECT):
                            next_copy(m, k, n).start()

        @pl.when(is_last)
        def _():
            done = jnp.concatenate([x_out[m, k] for k in range(CHUNKS)], axis=1).astype(F32)
            for b in range(SEQ):
                piece = done[8 * b : 8 * b + 8]
                fin_out[m, b] = jnp.concatenate([piece[:, :128], piece[:, 128:]], axis=0).astype(BF16)

            @pl.when(is_own_out)
            def _():
                home_copy(m).start()

                def send(k, inner):
                    fin_copy(m, (i + k) % SEQ).start()
                    return inner

                lax.fori_loop(1, SEQ, send, 0)

            @pl.when(jnp.logical_not(is_own_out))
            def _():
                for b in range(SEQ):
                    fin_copy(m, b).start()

        return carry

    def fin_copy(m, b):
        return remote(
            fin_out.at[m, b], fin_in.at[c, m], fin_send.at[m], fin_recv.at[c, m], (i // PIPE, i % PIPE, b)
        )

    def home_copy(m):
        return pltpu.make_async_copy(fin_out.at[m, i], fin_in.at[c, m], fin_recv.at[c, m])

    lax.fori_loop(0, MICRO, patch_step, 0)

    def left(ref, sem):
        remote(ref, ref, sem, recv_sem.at[0, 0, 0, 0], (c, s, sib)).wait_send()

    def drain_pos(k, carry):
        pos_copy(k).wait_send()
        return carry

    lax.fori_loop(1, SEQ, drain_pos, 0)

    for m in range(MICRO):
        left(x_buf.at[0, 0], fwd_sem.at[m])


        @pl.when(is_first)
        def _():
            left(x_buf.at[0, 0, :, pl.ds(0, CHIPS - 1)], plane_sem.at[m])

        @pl.when(s > 0)
        def _():
            left(x_buf.at[0, 0, :, pl.ds(0, CHIPS - N_DIRECT)], plane_sem.at[m])

        @pl.when(s < PIPE - 1)
        def _():
            left(x_buf.at[0, 0, :, pl.ds(0, N_DIRECT)], next_sem.at[m])

        @pl.when(jnp.logical_and(is_last, is_own_out))
        def _():
            left(fin_out.at[m, pl.ds(0, SEQ - 1)], fin_send.at[m])

        @pl.when(jnp.logical_and(is_last, jnp.logical_not(is_own_out)))
        def _():
            left(fin_out.at[m], fin_send.at[m])

    guided = []
    for m in range(MICRO):
        for branch in range(2):
            here = fin_in.at[branch, m]
            remote(here, here, fin_send.at[m], fin_recv.at[branch, m], (c, s, sib)).wait_recv()
        cond = fin_in[0, m].astype(F32)
        uncond = fin_in[1, m].astype(F32)
        piece = uncond + GUIDANCE * (cond - uncond)
        guided.append(jnp.concatenate([piece[:8], piece[8:]], axis=1))
    guided = jnp.concatenate(guided, axis=0).astype(BF16)
    out_ref[...] = jnp.dot(from_sorted, guided, preferred_element_type=F32).astype(BF16)


def body(hidden, modulation, qkv_weight, stale_cache, patch_of):
    vmem, dma = pltpu.VMEM, pltpu.SemaphoreType.DMA
    hbm = pl.BlockSpec(memory_space=pl.ANY)
    return pl.pallas_call(
        kernel,
        out_shape=jax.ShapeDtypeStruct((32, COLS), BF16),
        in_specs=[hbm, hbm, hbm, hbm, pl.BlockSpec(memory_space=pltpu.VMEM)],
        out_specs=pl.BlockSpec(memory_space=pltpu.VMEM),
        scratch_shapes=[
            vmem((2 * MICRO, 2, CHUNKS, CHIPS, ROWS, CW), BF16),
            vmem((SEQ, 3, COLS, COLS), BF16),
            vmem((32, D), BF16),
            vmem((96, 128), F32),
            vmem((2, 512, COLS), BF16),
            vmem((32, D), F32),
            vmem((2, 512, COLS), BF16),
            vmem((3, ROWS, COLS), F32),
            vmem((ROWS, 128), F32),
            vmem((ROWS, 128), F32),
            vmem((3, 8, COLS), F32),
            vmem((3, 16, COLS), F32),
            vmem((SEQ, 8, 128), F32),
            vmem((MICRO, CHUNKS, ROWS, CW), BF16),
            vmem((MICRO, SEQ, 16, 128), BF16),
            vmem((2, MICRO, 16, 128), BF16),
            dma((3,)),
            dma((SEQ,)),
            dma((SEQ,)),
            dma((SEQ,)),
            dma((MICRO,)),
            dma((MICRO,)),
            dma((MICRO,)),
            dma((MICRO, 2, 4, CHUNKS)),
            dma((MICRO,)),
            dma((2, MICRO)),
        ],
        compiler_params=pltpu.CompilerParams(
            collective_id=0, has_side_effects=True, vmem_limit_bytes=56 * 2**20
        ),
        cost_estimate=pl.CostEstimate(flops=4 * 10**9, bytes_accessed=8 * 2**20, transcendentals=10**6),
        name="layers",
    )(hidden, modulation.reshape(96, 128), qkv_weight, stale_cache, patch_of.reshape(1, 32))


def solution(mesh):
    placed = (
        P("cfg", "seq", None),
        P("pipe", None, None),
        P("pipe", None, None, "seq"),
        P("cfg", "pipe", None, None, "seq"),
        P("seq"),
    )
    return jax.shard_map(
        body, mesh=mesh, in_specs=placed, out_specs=P("seq", ("cfg", "pipe")), check_vma=False
    )
```

```python
import functools

import jax
import jax.numpy as jnp
from jax import lax
from jax.experimental import pallas as pl
from jax.experimental.pallas import tpu as pltpu
from jax.sharding import PartitionSpec as P

F32 = jnp.float32
BF16 = jnp.bfloat16
MESH = pl.DeviceIdType.MESH

HD = 128
D = 4096
MICRO = 4
ROWS = 128
COLS = 256
SEQ = 16
PIPE = 8
GUIDANCE = 5.0
NORM_EPS = 1e-06
LOG2_E = 1.4426950408889634

OFFSETS = ((0, 0), (1, 1), (3, 1), (2, 1), (0, 1), (1, 0), (3, 0), (2, 0))
BACK = tuple(OFFSETS.index(((4 - dx) % 4, dy)) for dx, dy in OFFSETS)
CHIPS = 8
N_DIRECT = 4
GROUPS = ((0, 1), (1, N_DIRECT), (N_DIRECT, CHIPS - 2), (CHIPS - 2, CHIPS))
OWN, DIRECT, RELAY, FAR = 0, 1, 2, 3
RELAY_ORDER = (7, 5, 6, 4)
CHUNKS = 2
CW = COLS // CHUNKS


def kernel(
    hid_hbm, mod_hbm, w_hbm, stale_hbm, patch_ref, out_ref,
    x_buf, w_buf, hid, mod, stale, sorted_rows, kv, acc, sum1, sum2, colsum, shifted,
    pos_buf, x_out, fin_out, fin_in,
    load_sem, w_sem, pos_send, pos_recv, plane_sem, fwd_sem, next_sem, recv_sem, fin_send, fin_recv,
):
    c = lax.axis_index("cfg")
    s = lax.axis_index("pipe")
    i = lax.axis_index("seq")
    core = i % 2
    y = (i // 2) % 2
    x = i // 4
    is_first = s == 0
    is_last = s == PIPE - 1
    relay_flip = jnp.where(is_first, 0, 1)

    def at(n, other=0):
        dx, dy = OFFSETS[n]
        return (((x + dx) % 4) * 2 + (y + dy) % 2) * 2 + (core + other) % 2

    def source(side, n):
        return at(n, side + relay_flip if n > 0 else side)

    sib = at(0, 1)
    out_col = c * PIPE + s

    loads = [
        pltpu.make_async_copy(hid_hbm.at[0], hid, load_sem.at[0]),
        pltpu.make_async_copy(mod_hbm, mod, load_sem.at[1]),
        pltpu.make_async_copy(stale_hbm.at[0, 0], stale, load_sem.at[2]),
    ]

    def w_copy(b):
        return pltpu.make_async_copy(
            w_hbm.at[0, :, pl.ds(pl.multiple_of(b * COLS, COLS), COLS), :], w_buf.at[b], w_sem.at[b]
        )

    barrier = pltpu.get_barrier_semaphore()

    def greet(target):
        pl.semaphore_signal(barrier, inc=1, device_id=target, device_id_type=MESH)

    def greet_plane(k, carry):
        greet((c, s, (i + k) % SEQ))
        return carry

    lax.fori_loop(1, SEQ, greet_plane, 0)

    @pl.when(s > 0)
    def _():
        for n in range(N_DIRECT):
            greet((c, s - 1, at(n, 1 if n else 0)))

    for branch in range(2):
        is_self = jnp.logical_and(jnp.logical_and(c == branch, is_last), i == out_col)

        @pl.when(jnp.logical_not(is_self))
        def _():
            greet((branch, PIPE - 1, out_col))

    for load in loads:
        load.start()

    def start_w(b, carry):
        w_copy(b).start()
        return carry

    patch_row = jnp.broadcast_to(patch_ref[...].astype(F32), (32, 32))
    row32 = lax.broadcasted_iota(jnp.int32, (32, 32), 0)
    col32 = lax.broadcasted_iota(jnp.int32, (32, 32), 1)
    patch_col = jnp.sum(jnp.where(row32 == col32, patch_row, 0.0), axis=1, keepdims=True)
    same = jnp.where(patch_row == patch_col, 1.0, 0.0)
    rank_col = jnp.sum(jnp.where(col32 < row32, same, 0.0), axis=1, keepdims=True)
    rank_row = jnp.sum(jnp.where(row32 < col32, same, 0.0), axis=0, keepdims=True)
    pos_row = patch_row[0:1] * 8.0 + rank_row
    pos_col = patch_col * 8.0 + rank_col
    to_sorted = jnp.where(pos_row == row32.astype(F32), 1.0, 0.0).astype(BF16)
    from_sorted = jnp.where(pos_col == col32.astype(F32), 1.0, 0.0).astype(BF16)
    whole_pos = patch_col * float(ROWS) + rank_col + (i * 8).astype(F32)
    row128 = lax.broadcasted_iota(jnp.int32, (32, 128), 0)
    lane128 = lax.broadcasted_iota(jnp.int32, (32, 128), 1)
    placed = jnp.where(lane128 == row128 + (i % 4) * 32, whole_pos, 0.0)
    pos_buf[i] = jnp.broadcast_to(jnp.sum(placed, axis=0, keepdims=True), (8, 128))

    loads[0].wait()
    lax.fori_loop(0, SEQ, start_w, 0)

    @pl.when(is_first)
    def _():
        sorted_rows[...] = jnp.dot(to_sorted, hid[...], preferred_element_type=F32)
        for m in range(MICRO):
            for k in range(CHUNKS):
                pieces = [
                    sorted_rows[8 * m : 8 * m + 8, COLS * j + CW * k : COLS * j + CW * (k + 1)] for j in range(SEQ)
                ]
                x_buf[MICRO + m, 0, k, 0] = jnp.concatenate(pieces, axis=0).astype(BF16)

    is_own_out = jnp.logical_and(is_last, i == out_col)
    expected = (
        (SEQ - 1)
        + jnp.where(is_last, SEQ, N_DIRECT)
        - jnp.where(is_own_out, 1, 0)
    )
    pl.semaphore_wait(barrier, expected)

    def pos_copy(k):
        return pltpu.make_async_remote_copy(
            src_ref=pos_buf.at[i], dst_ref=pos_buf.at[i], send_sem=pos_send.at[k], recv_sem=pos_recv.at[i],
            device_id=(c, s, (i + k) % SEQ), device_id_type=MESH,
        )

    def pos_arrival(b):
        return pltpu.make_async_remote_copy(
            src_ref=pos_buf.at[b], dst_ref=pos_buf.at[b], send_sem=pos_send.at[0], recv_sem=pos_recv.at[b],
            device_id=(c, s, sib), device_id_type=MESH,
        )

    def slot_of(m):
        return m + jnp.where(is_first, MICRO, 0)

    def remote(src, dst, send, recv, target):
        return pltpu.make_async_remote_copy(
            src_ref=src, dst_ref=dst, send_sem=send, recv_sem=recv, device_id=target, device_id_type=MESH
        )

    def region(m, side, k, group):
        low, high = GROUPS[group]
        return x_buf.at[slot_of(m), side, k, pl.ds(low, high - low)]

    def plane_copy(m, k, n):
        slot = slot_of(m)
        there = BACK[n]
        group = DIRECT if there < N_DIRECT else RELAY if there < CHIPS - 2 else FAR
        return remote(
            x_buf.at[slot, 0, k, 0], x_buf.at[slot, 0, k, there],
            plane_sem.at[m], recv_sem.at[m, 0, group, k], (c, s, at(n, relay_flip)),
        )

    def fwd_copy(m, k, group):
        return remote(
            region(m, 0, k, group), region(m, 1, k, group), fwd_sem.at[m], recv_sem.at[m, 1, group, k], (c, s, sib)
        )

    def next_copy(m, k, n):
        return remote(
            x_out.at[m, k], x_buf.at[m, 0, k, BACK[n]],
            next_sem.at[m], recv_sem.at[m, 0, OWN if n == 0 else DIRECT, k], (c, s + 1, at(n, 1 if n else 0)),
        )

    def arrive(m, side, k, group):
        here = region(m, side, k, group)
        remote(here, here, fwd_sem.at[m], recv_sem.at[m, side, group, k], (c, s, sib)).wait_recv()

    def take(m, *groups):
        for k in range(CHUNKS):
            for group in groups:
                arrive(m, 0, k, group)
                fwd_copy(m, k, group).start()

    def take_sib(m, *groups):
        for group in groups:
            for k in range(CHUNKS):
                arrive(m, 1, k, group)

    def spread(m):
        for k in range(CHUNKS):
            @pl.when(s > 0)
            def _():
                arrive(m, 0, k, OWN)

            for n in RELAY_ORDER:
                plane_copy(m, k, n).start()
            fwd_copy(m, k, OWN).start()

    def spread_first(m):
        @pl.when(is_first)
        def _():
            for k in range(CHUNKS):
                for n in range(*GROUPS[DIRECT]):
                    plane_copy(m, k, n).start()
            spread(m)

    spread_first(0)

    def send_pos(k, carry):
        pos_copy(k).start()
        return carry

    lax.fori_loop(1, SEQ, send_pos, 0)

    loads[1].wait()
    colsum[...] = jnp.zeros_like(colsum)
    shifted[...] = jnp.zeros_like(shifted)

    def fold(b, carry):
        w_copy(b).wait()
        gain = jnp.concatenate(
            [jnp.broadcast_to(1.0 + mod[pl.ds(32 + 2 * b + n, 1), :], (128, 128)).T for n in range(2)], axis=0
        )
        gain = jnp.concatenate([gain, gain], axis=1)
        shift = jnp.broadcast_to(
            jnp.concatenate([mod[pl.ds(2 * b + n, 1), :] for n in range(2)], axis=1), (8, COLS)
        )
        shift_high = shift.astype(BF16)
        shift_low = (shift - shift_high.astype(F32)).astype(BF16)
        shift_both = jnp.concatenate([shift_high, shift_low], axis=0)
        ones = jnp.ones((8, COLS), BF16)
        for t in range(3):
            raw = w_buf[b, t]
            shifted[t] += jnp.dot(shift_both, raw, preferred_element_type=F32)
            scaled = (raw.astype(F32) * gain).astype(BF16)
            w_buf[b, t] = scaled
            colsum[t] += jnp.dot(ones, scaled, preferred_element_type=F32)
        return carry

    lax.fori_loop(0, SEQ // 2, fold, 0)

    spread_first(1)

    lax.fori_loop(SEQ // 2, SEQ, fold, 0)

    spread_first(2)

    loads[2].wait()

    def wait_pos(k, carry):
        pos_arrival((i + k) % SEQ).wait_recv()
        return carry

    lax.fori_loop(1, SEQ, wait_pos, 0)
    pos_all = jnp.concatenate(
        [sum(pos_buf[4 * g + n, 0:1, :] for n in range(4)) for g in range(4)], axis=1
    )
    for g in range(4):
        rows = lax.broadcasted_iota(jnp.int32, (128, 512), 0).astype(F32) + float(128 * g)
        pick = jnp.where(pos_all == rows, 1.0, 0.0).astype(BF16)
        for t in range(2):
            kv[t, 128 * g : 128 * g + 128, :] = jnp.dot(
                pick, stale[t], preferred_element_type=F32
            ).astype(BF16)

    spread_first(3)

    @pl.when(s > 0)
    def _():
        spread(0)

    def block(m, side, n):
        return jnp.concatenate([x_buf[m, side, k, n] for k in range(CHUNKS)], axis=1)

    def project(m, side, low, high):
        parts = [block(m, side, n) for n in range(low, high)]
        rows = [source(side, n) for n in range(low, high)]
        fresh = side == 0 and low == 0
        for t in range(3):
            total = sum(jnp.dot(part, w_buf[b, t], preferred_element_type=F32) for part, b in zip(parts, rows))
            acc[t] = total if fresh else acc[t] + total
        one = jnp.zeros((ROWS, 128), F32) if fresh else sum1[...]
        two = jnp.zeros((ROWS, 128), F32) if fresh else sum2[...]
        for part in parts:
            wide = part.astype(F32)
            square = wide * wide
            one = one + wide[:, :128] + wide[:, 128:]
            two = two + square[:, :128] + square[:, 128:]
        sum1[...] = one
        sum2[...] = two

    def project_half(m, side, k, low, high):
        pairs = [(n, n + 1) for n in range(low, high, 2)]
        parts = [jnp.concatenate([x_buf[m, side, k, n] for n in pair], axis=1) for pair in pairs]
        rows = slice(CW * k, CW * (k + 1))
        for t in range(3):
            total = acc[t]
            for part, pair in zip(parts, pairs):
                weight = jnp.concatenate([w_buf[source(side, n), t, rows, :] for n in pair], axis=0)
                total = total + jnp.dot(part, weight, preferred_element_type=F32)
            acc[t] = total
        one = sum1[...]
        two = sum2[...]
        for part in parts:
            wide = part.astype(F32)
            square = wide * wide
            one = one + wide[:, :128] + wide[:, 128:]
            two = two + square[:, :128] + square[:, 128:]
        sum1[...] = one
        sum2[...] = two

    scaling = LOG2_E / (HD ** 0.5)

    def patch_step(m, carry):
        @pl.when(is_first)
        def _():
            take(m, DIRECT, RELAY, FAR)
            take_sib(m, OWN, DIRECT, RELAY, FAR)

            def where_is(b):
                chip = 0
                for n in range(1, CHIPS):
                    chip = chip + jnp.where(at(n) // 2 == b // 2, n, 0)
                return (b + core) % 2, chip

            homes = [where_is(b) for b in range(SEQ)]
            for n in range(CHIPS):
                span = pl.ds(pl.multiple_of((at(n) // 2) * 16, 16), 16)
                for k in range(CHUNKS):
                    pieces = [x_buf[MICRO + m, side, k, chip, span, :].astype(F32) for side, chip in homes]
                    for half in range(2):
                        x_buf[m, (half + core) % 2, k, n] = jnp.concatenate(
                            [piece[8 * half : 8 * half + 8] for piece in pieces], axis=0
                        ).astype(BF16)

        @pl.when(s > 0)
        def _():
            @pl.when(m < MICRO - 1)
            def _():
                spread(m + 1)

            take(m, DIRECT, RELAY, FAR)

        project(m, 0, 0, N_DIRECT)
        project(m, 0, N_DIRECT, CHIPS)

        @pl.when(s > 0)
        def _():
            take_sib(m, OWN, DIRECT)

        project(m, 1, 0, N_DIRECT)

        for k in range(CHUNKS):
            @pl.when(s > 0)
            def _():
                arrive(m, 1, k, RELAY)
                arrive(m, 1, k, FAR)

            project_half(m, 1, k, N_DIRECT, CHIPS)

        mean = jnp.sum(sum1[...], axis=1, keepdims=True) * (1.0 / D)
        var = jnp.sum(sum2[...], axis=1, keepdims=True) * (1.0 / D) - mean * mean
        inv = lax.rsqrt(var + NORM_EPS)

        def finish(t):
            bias = shifted[t, 0:1] + shifted[t, 8:9]
            return (inv * (acc[t] - mean * colsum[t, 0:1]) + bias).astype(BF16)

        query = finish(0)
        rows = pl.ds(pl.multiple_of(m * ROWS, ROWS), ROWS)
        kv[0, rows, :] = finish(1)
        kv[1, rows, :] = finish(2)
        old = block(m, 0, 0)
        for h in range(2):
            cols = slice(h * HD, (h + 1) * HD)
            scores = lax.dot_general(
                query[:, cols], kv[0, :, cols], (((1,), (1,)), ((), ())), preferred_element_type=F32
            )
            top = jnp.max(scores, axis=1, keepdims=True)
            weights = jnp.exp2((scores - top) * scaling)
            norm = 1.0 / jnp.sum(weights, axis=1, keepdims=True)
            mixed = jnp.dot(weights.astype(BF16), kv[1, :, cols], preferred_element_type=F32) * norm
            mixed = mixed.astype(BF16).astype(F32)
            fresh = (old[:, cols].astype(F32) + mod[pl.ds(64 + 2 * i + h, 1), :] * mixed).astype(BF16)
            x_out[m, h] = fresh

            @pl.when(s < PIPE - 1)
            def _():
                next_copy(m, h, 0).start()
                if h == 1:
                    for k in range(CHUNKS):
                        for n in range(1, N_DIRECT):
                            next_copy(m, k, n).start()

        @pl.when(is_last)
        def _():
            done = jnp.concatenate([x_out[m, k] for k in range(CHUNKS)], axis=1).astype(F32)
            for b in range(SEQ):
                piece = done[8 * b : 8 * b + 8]
                fin_out[m, b] = jnp.concatenate([piece[:, :128], piece[:, 128:]], axis=0).astype(BF16)

            @pl.when(is_own_out)
            def _():
                home_copy(m).start()

                def send(k, inner):
                    fin_copy(m, (i + k) % SEQ).start()
                    return inner

                lax.fori_loop(1, SEQ, send, 0)

            @pl.when(jnp.logical_not(is_own_out))
            def _():
                for b in range(SEQ):
                    fin_copy(m, b).start()

        return carry

    def fin_copy(m, b):
        return remote(
            fin_out.at[m, b], fin_in.at[c, m], fin_send.at[m], fin_recv.at[c, m], (i // PIPE, i % PIPE, b)
        )

    def home_copy(m):
        return pltpu.make_async_copy(fin_out.at[m, i], fin_in.at[c, m], fin_recv.at[c, m])

    lax.fori_loop(0, MICRO, patch_step, 0)

    def left(ref, sem):
        remote(ref, ref, sem, recv_sem.at[0, 0, 0, 0], (c, s, sib)).wait_send()

    def drain_pos(k, carry):
        pos_copy(k).wait_send()
        return carry

    lax.fori_loop(1, SEQ, drain_pos, 0)

    for m in range(MICRO):
        left(x_buf.at[0, 0], fwd_sem.at[m])


        @pl.when(is_first)
        def _():
            left(x_buf.at[0, 0, :, pl.ds(0, CHIPS - 1)], plane_sem.at[m])

        @pl.when(s > 0)
        def _():
            left(x_buf.at[0, 0, :, pl.ds(0, CHIPS - N_DIRECT)], plane_sem.at[m])

        @pl.when(s < PIPE - 1)
        def _():
            left(x_buf.at[0, 0, :, pl.ds(0, N_DIRECT)], next_sem.at[m])

        @pl.when(jnp.logical_and(is_last, is_own_out))
        def _():
            left(fin_out.at[m, pl.ds(0, SEQ - 1)], fin_send.at[m])

        @pl.when(jnp.logical_and(is_last, jnp.logical_not(is_own_out)))
        def _():
            left(fin_out.at[m], fin_send.at[m])

    guided = []
    for m in range(MICRO):
        for branch in range(2):
            here = fin_in.at[branch, m]
            remote(here, here, fin_send.at[m], fin_recv.at[branch, m], (c, s, sib)).wait_recv()
        cond = fin_in[0, m].astype(F32)
        uncond = fin_in[1, m].astype(F32)
        piece = uncond + GUIDANCE * (cond - uncond)
        guided.append(jnp.concatenate([piece[:8], piece[8:]], axis=1))
    guided = jnp.concatenate(guided, axis=0).astype(BF16)
    out_ref[...] = jnp.dot(from_sorted, guided, preferred_element_type=F32).astype(BF16)


def body(hidden, modulation, qkv_weight, stale_cache, patch_of):
    vmem, dma = pltpu.VMEM, pltpu.SemaphoreType.DMA
    hbm = pl.BlockSpec(memory_space=pl.ANY)
    return pl.pallas_call(
        kernel,
        out_shape=jax.ShapeDtypeStruct((32, COLS), BF16),
        in_specs=[hbm, hbm, hbm, hbm, pl.BlockSpec(memory_space=pltpu.VMEM)],
        out_specs=pl.BlockSpec(memory_space=pltpu.VMEM),
        scratch_shapes=[
            vmem((2 * MICRO, 2, CHUNKS, CHIPS, ROWS, CW), BF16),
            vmem((SEQ, 3, COLS, COLS), BF16),
            vmem((32, D), BF16),
            vmem((96, 128), F32),
            vmem((2, 512, COLS), BF16),
            vmem((32, D), F32),
            vmem((2, 512, COLS), BF16),
            vmem((3, ROWS, COLS), F32),
            vmem((ROWS, 128), F32),
            vmem((ROWS, 128), F32),
            vmem((3, 8, COLS), F32),
            vmem((3, 16, COLS), F32),
            vmem((SEQ, 8, 128), F32),
            vmem((MICRO, CHUNKS, ROWS, CW), BF16),
            vmem((MICRO, SEQ, 16, 128), BF16),
            vmem((2, MICRO, 16, 128), BF16),
            dma((3,)),
            dma((SEQ,)),
            dma((SEQ,)),
            dma((SEQ,)),
            dma((MICRO,)),
            dma((MICRO,)),
            dma((MICRO,)),
            dma((MICRO, 2, 4, CHUNKS)),
            dma((MICRO,)),
            dma((2, MICRO)),
        ],
        compiler_params=pltpu.CompilerParams(
            collective_id=0, has_side_effects=True, vmem_limit_bytes=56 * 2**20
        ),
        cost_estimate=pl.CostEstimate(flops=4 * 10**9, bytes_accessed=8 * 2**20, transcendentals=10**6),
        name="layers",
    )(hidden, modulation.reshape(96, 128), qkv_weight, stale_cache, patch_of.reshape(1, 32))


def solution(mesh):
    placed = (
        P("cfg", "seq", None),
        P("pipe", None, None),
        P("pipe", None, None, "seq"),
        P("cfg", "pipe", None, None, "seq"),
        P("seq"),
    )
    return jax.shard_map(
        body, mesh=mesh, in_specs=placed, out_specs=P("seq", ("cfg", "pipe")), check_vma=False
    )
```

```python
import functools

import jax
import jax.numpy as jnp
from jax import lax
from jax.experimental import pallas as pl
from jax.experimental.pallas import tpu as pltpu
from jax.sharding import PartitionSpec as P

F32 = jnp.float32
BF16 = jnp.bfloat16
MESH = pl.DeviceIdType.MESH

HD = 128
D = 4096
MICRO = 4
ROWS = 128
COLS = 256
SEQ = 16
PIPE = 8
GUIDANCE = 5.0
NORM_EPS = 1e-06
LOG2_E = 1.4426950408889634

OFFSETS = ((0, 0), (1, 1), (3, 1), (2, 1), (0, 1), (1, 0), (3, 0), (2, 0))
BACK = tuple(OFFSETS.index(((4 - dx) % 4, dy)) for dx, dy in OFFSETS)
CHIPS = 8
N_DIRECT = 4
GROUPS = ((0, 1), (1, N_DIRECT), (N_DIRECT, CHIPS - 2), (CHIPS - 2, CHIPS))
OWN, DIRECT, RELAY, FAR = 0, 1, 2, 3
RELAY_ORDER = (7, 5, 6, 4)
CHUNKS = 2
CW = COLS // CHUNKS


def kernel(
    hid_hbm, mod_hbm, w_hbm, stale_hbm, patch_ref, out_ref,
    x_buf, w_buf, hid, mod, stale, sorted_rows, kv, acc, sum1, sum2, colsum, shifted,
    pos_buf, x_out, fin_out, fin_in,
    load_sem, w_sem, pos_send, pos_recv, plane_sem, fwd_sem, next_sem, recv_sem, fin_send, fin_recv,
):
    c = lax.axis_index("cfg")
    s = lax.axis_index("pipe")
    i = lax.axis_index("seq")
    core = i % 2
    y = (i // 2) % 2
    x = i // 4
    is_first = s == 0
    is_last = s == PIPE - 1
    relay_flip = jnp.where(is_first, 0, 1)

    def at(n, other=0):
        dx, dy = OFFSETS[n]
        return (((x + dx) % 4) * 2 + (y + dy) % 2) * 2 + (core + other) % 2

    def source(side, n):
        return at(n, side + relay_flip if n > 0 else side)

    sib = at(0, 1)
    out_col = c * PIPE + s

    loads = [
        pltpu.make_async_copy(hid_hbm.at[0], hid, load_sem.at[0]),
        pltpu.make_async_copy(mod_hbm, mod, load_sem.at[1]),
        pltpu.make_async_copy(stale_hbm.at[0, 0], stale, load_sem.at[2]),
    ]

    def w_copy(b):
        return pltpu.make_async_copy(
            w_hbm.at[0, :, pl.ds(pl.multiple_of(b * COLS, COLS), COLS), :], w_buf.at[b], w_sem.at[b]
        )

    barrier = pltpu.get_barrier_semaphore()

    def greet(target):
        pl.semaphore_signal(barrier, inc=1, device_id=target, device_id_type=MESH)

    def greet_plane(k, carry):
        greet((c, s, (i + k) % SEQ))
        return carry

    lax.fori_loop(1, SEQ, greet_plane, 0)

    @pl.when(s > 0)
    def _():
        for n in range(N_DIRECT):
            greet((c, s - 1, at(n, 1 if n else 0)))

    for branch in range(2):
        is_self = jnp.logical_and(jnp.logical_and(c == branch, is_last), i == out_col)

        @pl.when(jnp.logical_not(is_self))
        def _():
            greet((branch, PIPE - 1, out_col))

    for load in loads:
        load.start()

    def start_w(b, carry):
        w_copy(b).start()
        return carry

    patch_row = jnp.broadcast_to(patch_ref[...].astype(F32), (32, 32))
    row32 = lax.broadcasted_iota(jnp.int32, (32, 32), 0)
    col32 = lax.broadcasted_iota(jnp.int32, (32, 32), 1)
    patch_col = jnp.sum(jnp.where(row32 == col32, patch_row, 0.0), axis=1, keepdims=True)
    same = jnp.where(patch_row == patch_col, 1.0, 0.0)
    rank_col = jnp.sum(jnp.where(col32 < row32, same, 0.0), axis=1, keepdims=True)
    rank_row = jnp.sum(jnp.where(row32 < col32, same, 0.0), axis=0, keepdims=True)
    pos_row = patch_row[0:1] * 8.0 + rank_row
    pos_col = patch_col * 8.0 + rank_col
    to_sorted = jnp.where(pos_row == row32.astype(F32), 1.0, 0.0).astype(BF16)
    from_sorted = jnp.where(pos_col == col32.astype(F32), 1.0, 0.0).astype(BF16)
    whole_pos = patch_col * float(ROWS) + rank_col + (i * 8).astype(F32)
    row128 = lax.broadcasted_iota(jnp.int32, (32, 128), 0)
    lane128 = lax.broadcasted_iota(jnp.int32, (32, 128), 1)
    placed = jnp.where(lane128 == row128 + (i % 4) * 32, whole_pos, 0.0)
    pos_buf[i] = jnp.broadcast_to(jnp.sum(placed, axis=0, keepdims=True), (8, 128))

    loads[0].wait()
    lax.fori_loop(0, SEQ, start_w, 0)

    @pl.when(is_first)
    def _():
        sorted_rows[...] = jnp.dot(to_sorted, hid[...], preferred_element_type=F32)
        for m in range(MICRO):
            for k in range(CHUNKS):
                pieces = [
                    sorted_rows[8 * m : 8 * m + 8, COLS * j + CW * k : COLS * j + CW * (k + 1)] for j in range(SEQ)
                ]
                x_buf[MICRO + m, 0, k, 0] = jnp.concatenate(pieces, axis=0).astype(BF16)

    is_own_out = jnp.logical_and(is_last, i == out_col)
    expected = (
        (SEQ - 1)
        + jnp.where(is_last, SEQ, N_DIRECT)
        - jnp.where(is_own_out, 1, 0)
    )
    pl.semaphore_wait(barrier, expected)

    def pos_copy(k):
        return pltpu.make_async_remote_copy(
            src_ref=pos_buf.at[i], dst_ref=pos_buf.at[i], send_sem=pos_send.at[k], recv_sem=pos_recv.at[i],
            device_id=(c, s, (i + k) % SEQ), device_id_type=MESH,
        )

    def pos_arrival(b):
        return pltpu.make_async_remote_copy(
            src_ref=pos_buf.at[b], dst_ref=pos_buf.at[b], send_sem=pos_send.at[0], recv_sem=pos_recv.at[b],
            device_id=(c, s, sib), device_id_type=MESH,
        )

    def slot_of(m):
        return m + jnp.where(is_first, MICRO, 0)

    def remote(src, dst, send, recv, target):
        return pltpu.make_async_remote_copy(
            src_ref=src, dst_ref=dst, send_sem=send, recv_sem=recv, device_id=target, device_id_type=MESH
        )

    def region(m, side, k, group):
        low, high = GROUPS[group]
        return x_buf.at[slot_of(m), side, k, pl.ds(low, high - low)]

    def plane_copy(m, k, n):
        slot = slot_of(m)
        there = BACK[n]
        group = DIRECT if there < N_DIRECT else RELAY if there < CHIPS - 2 else FAR
        return remote(
            x_buf.at[slot, 0, k, 0], x_buf.at[slot, 0, k, there],
            plane_sem.at[m], recv_sem.at[m, 0, group, k], (c, s, at(n, relay_flip)),
        )

    def fwd_copy(m, k, group):
        return remote(
            region(m, 0, k, group), region(m, 1, k, group), fwd_sem.at[m], recv_sem.at[m, 1, group, k], (c, s, sib)
        )

    def next_copy(m, k, n):
        return remote(
            x_out.at[m, k], x_buf.at[m, 0, k, BACK[n]],
            next_sem.at[m], recv_sem.at[m, 0, OWN if n == 0 else DIRECT, k], (c, s + 1, at(n, 1 if n else 0)),
        )

    def arrive(m, side, k, group):
        here = region(m, side, k, group)
        remote(here, here, fwd_sem.at[m], recv_sem.at[m, side, group, k], (c, s, sib)).wait_recv()

    def take(m, *groups):
        for k in range(CHUNKS):
            for group in groups:
                arrive(m, 0, k, group)
                fwd_copy(m, k, group).start()

    def take_sib(m, *groups):
        for group in groups:
            for k in range(CHUNKS):
                arrive(m, 1, k, group)

    def spread(m):
        for k in range(CHUNKS):
            @pl.when(s > 0)
            def _():
                arrive(m, 0, k, OWN)

            for n in RELAY_ORDER:
                plane_copy(m, k, n).start()
        for k in range(CHUNKS):
            fwd_copy(m, k, OWN).start()

    def spread_first(m):
        @pl.when(is_first)
        def _():
            for k in range(CHUNKS):
                for n in range(*GROUPS[DIRECT]):
                    plane_copy(m, k, n).start()
            spread(m)

    spread_first(0)

    def send_pos(k, carry):
        pos_copy(k).start()
        return carry

    lax.fori_loop(1, SEQ, send_pos, 0)

    loads[1].wait()
    colsum[...] = jnp.zeros_like(colsum)
    shifted[...] = jnp.zeros_like(shifted)

    def fold(b, carry):
        w_copy(b).wait()
        gain = jnp.concatenate(
            [jnp.broadcast_to(1.0 + mod[pl.ds(32 + 2 * b + n, 1), :], (128, 128)).T for n in range(2)], axis=0
        )
        gain = jnp.concatenate([gain, gain], axis=1)
        shift = jnp.broadcast_to(
            jnp.concatenate([mod[pl.ds(2 * b + n, 1), :] for n in range(2)], axis=1), (8, COLS)
        )
        shift_high = shift.astype(BF16)
        shift_low = (shift - shift_high.astype(F32)).astype(BF16)
        shift_both = jnp.concatenate([shift_high, shift_low], axis=0)
        ones = jnp.ones((8, COLS), BF16)
        for t in range(3):
            raw = w_buf[b, t]
            shifted[t] += jnp.dot(shift_both, raw, preferred_element_type=F32)
            scaled = (raw.astype(F32) * gain).astype(BF16)
            w_buf[b, t] = scaled
            colsum[t] += jnp.dot(ones, scaled, preferred_element_type=F32)
        return carry

    lax.fori_loop(0, SEQ // 2, fold, 0)

    spread_first(1)

    lax.fori_loop(SEQ // 2, SEQ, fold, 0)

    spread_first(2)

    loads[2].wait()

    def wait_pos(k, carry):
        pos_arrival((i + k) % SEQ).wait_recv()
        return carry

    lax.fori_loop(1, SEQ, wait_pos, 0)
    pos_all = jnp.concatenate(
        [sum(pos_buf[4 * g + n, 0:1, :] for n in range(4)) for g in range(4)], axis=1
    )
    for g in range(4):
        rows = lax.broadcasted_iota(jnp.int32, (128, 512), 0).astype(F32) + float(128 * g)
        pick = jnp.where(pos_all == rows, 1.0, 0.0).astype(BF16)
        for t in range(2):
            kv[t, 128 * g : 128 * g + 128, :] = jnp.dot(
                pick, stale[t], preferred_element_type=F32
            ).astype(BF16)

    spread_first(3)

    @pl.when(s > 0)
    def _():
        spread(0)

    def block(m, side, n):
        return jnp.concatenate([x_buf[m, side, k, n] for k in range(CHUNKS)], axis=1)

    def project(m, side, low, high):
        parts = [block(m, side, n) for n in range(low, high)]
        rows = [source(side, n) for n in range(low, high)]
        fresh = side == 0 and low == 0
        for t in range(3):
            total = sum(jnp.dot(part, w_buf[b, t], preferred_element_type=F32) for part, b in zip(parts, rows))
            acc[t] = total if fresh else acc[t] + total
        one = jnp.zeros((ROWS, 128), F32) if fresh else sum1[...]
        two = jnp.zeros((ROWS, 128), F32) if fresh else sum2[...]
        for part in parts:
            wide = part.astype(F32)
            square = wide * wide
            one = one + wide[:, :128] + wide[:, 128:]
            two = two + square[:, :128] + square[:, 128:]
        sum1[...] = one
        sum2[...] = two

    def project_half(m, side, k, low, high):
        pairs = [(n, n + 1) for n in range(low, high, 2)]
        parts = [jnp.concatenate([x_buf[m, side, k, n] for n in pair], axis=1) for pair in pairs]
        rows = slice(CW * k, CW * (k + 1))
        for t in range(3):
            total = acc[t]
            for part, pair in zip(parts, pairs):
                weight = jnp.concatenate([w_buf[source(side, n), t, rows, :] for n in pair], axis=0)
                total = total + jnp.dot(part, weight, preferred_element_type=F32)
            acc[t] = total
        one = sum1[...]
        two = sum2[...]
        for part in parts:
            wide = part.astype(F32)
            square = wide * wide
            one = one + wide[:, :128] + wide[:, 128:]
            two = two + square[:, :128] + square[:, 128:]
        sum1[...] = one
        sum2[...] = two

    scaling = LOG2_E / (HD ** 0.5)

    def patch_step(m, carry):
        @pl.when(is_first)
        def _():
            take(m, DIRECT, RELAY, FAR)
            take_sib(m, OWN, DIRECT, RELAY, FAR)

            def where_is(b):
                chip = 0
                for n in range(1, CHIPS):
                    chip = chip + jnp.where(at(n) // 2 == b // 2, n, 0)
                return (b + core) % 2, chip

            homes = [where_is(b) for b in range(SEQ)]
            for n in range(CHIPS):
                span = pl.ds(pl.multiple_of((at(n) // 2) * 16, 16), 16)
                for k in range(CHUNKS):
                    pieces = [x_buf[MICRO + m, side, k, chip, span, :].astype(F32) for side, chip in homes]
                    for half in range(2):
                        x_buf[m, (half + core) % 2, k, n] = jnp.concatenate(
                            [piece[8 * half : 8 * half + 8] for piece in pieces], axis=0
                        ).astype(BF16)

        @pl.when(s > 0)
        def _():
            @pl.when(m < MICRO - 1)
            def _():
                spread(m + 1)

            take(m, DIRECT, RELAY, FAR)

        project(m, 0, 0, N_DIRECT)
        project(m, 0, N_DIRECT, CHIPS)

        @pl.when(s > 0)
        def _():
            take_sib(m, OWN, DIRECT)

        project(m, 1, 0, N_DIRECT)

        for k in range(CHUNKS):
            @pl.when(s > 0)
            def _():
                arrive(m, 1, k, RELAY)
                arrive(m, 1, k, FAR)

            project_half(m, 1, k, N_DIRECT, CHIPS)

        mean = jnp.sum(sum1[...], axis=1, keepdims=True) * (1.0 / D)
        var = jnp.sum(sum2[...], axis=1, keepdims=True) * (1.0 / D) - mean * mean
        inv = lax.rsqrt(var + NORM_EPS)

        def finish(t):
            bias = shifted[t, 0:1] + shifted[t, 8:9]
            return (inv * (acc[t] - mean * colsum[t, 0:1]) + bias).astype(BF16)

        query = finish(0)
        rows = pl.ds(pl.multiple_of(m * ROWS, ROWS), ROWS)
        kv[0, rows, :] = finish(1)
        kv[1, rows, :] = finish(2)
        old = block(m, 0, 0)
        for h in range(2):
            cols = slice(h * HD, (h + 1) * HD)
            scores = lax.dot_general(
                query[:, cols], kv[0, :, cols], (((1,), (1,)), ((), ())), preferred_element_type=F32
            )
            top = jnp.max(scores, axis=1, keepdims=True)
            weights = jnp.exp2((scores - top) * scaling)
            norm = 1.0 / jnp.sum(weights, axis=1, keepdims=True)
            mixed = jnp.dot(weights.astype(BF16), kv[1, :, cols], preferred_element_type=F32) * norm
            mixed = mixed.astype(BF16).astype(F32)
            fresh = (old[:, cols].astype(F32) + mod[pl.ds(64 + 2 * i + h, 1), :] * mixed).astype(BF16)
            x_out[m, h] = fresh

            @pl.when(s < PIPE - 1)
            def _():
                next_copy(m, h, 0).start()
                if h == 1:
                    for k in range(CHUNKS):
                        for n in range(1, N_DIRECT):
                            next_copy(m, k, n).start()

        @pl.when(is_last)
        def _():
            done = jnp.concatenate([x_out[m, k] for k in range(CHUNKS)], axis=1).astype(F32)
            for b in range(SEQ):
                piece = done[8 * b : 8 * b + 8]
                fin_out[m, b] = jnp.concatenate([piece[:, :128], piece[:, 128:]], axis=0).astype(BF16)

            @pl.when(is_own_out)
            def _():
                home_copy(m).start()

                def send(k, inner):
                    fin_copy(m, (i + k) % SEQ).start()
                    return inner

                lax.fori_loop(1, SEQ, send, 0)

            @pl.when(jnp.logical_not(is_own_out))
            def _():
                for b in range(SEQ):
                    fin_copy(m, b).start()

        return carry

    def fin_copy(m, b):
        return remote(
            fin_out.at[m, b], fin_in.at[c, m], fin_send.at[m], fin_recv.at[c, m], (i // PIPE, i % PIPE, b)
        )

    def home_copy(m):
        return pltpu.make_async_copy(fin_out.at[m, i], fin_in.at[c, m], fin_recv.at[c, m])

    lax.fori_loop(0, MICRO, patch_step, 0)

    def left(ref, sem):
        remote(ref, ref, sem, recv_sem.at[0, 0, 0, 0], (c, s, sib)).wait_send()

    def drain_pos(k, carry):
        pos_copy(k).wait_send()
        return carry

    lax.fori_loop(1, SEQ, drain_pos, 0)

    for m in range(MICRO):
        left(x_buf.at[0, 0], fwd_sem.at[m])


        @pl.when(is_first)
        def _():
            left(x_buf.at[0, 0, :, pl.ds(0, CHIPS - 1)], plane_sem.at[m])

        @pl.when(s > 0)
        def _():
            left(x_buf.at[0, 0, :, pl.ds(0, CHIPS - N_DIRECT)], plane_sem.at[m])

        @pl.when(s < PIPE - 1)
        def _():
            left(x_buf.at[0, 0, :, pl.ds(0, N_DIRECT)], next_sem.at[m])

        @pl.when(jnp.logical_and(is_last, is_own_out))
        def _():
            left(fin_out.at[m, pl.ds(0, SEQ - 1)], fin_send.at[m])

        @pl.when(jnp.logical_and(is_last, jnp.logical_not(is_own_out)))
        def _():
            left(fin_out.at[m], fin_send.at[m])

    guided = []
    for m in range(MICRO):
        for branch in range(2):
            here = fin_in.at[branch, m]
            remote(here, here, fin_send.at[m], fin_recv.at[branch, m], (c, s, sib)).wait_recv()
        cond = fin_in[0, m].astype(F32)
        uncond = fin_in[1, m].astype(F32)
        piece = uncond + GUIDANCE * (cond - uncond)
        guided.append(jnp.concatenate([piece[:8], piece[8:]], axis=1))
    guided = jnp.concatenate(guided, axis=0).astype(BF16)
    out_ref[...] = jnp.dot(from_sorted, guided, preferred_element_type=F32).astype(BF16)


def body(hidden, modulation, qkv_weight, stale_cache, patch_of):
    vmem, dma = pltpu.VMEM, pltpu.SemaphoreType.DMA
    hbm = pl.BlockSpec(memory_space=pl.ANY)
    return pl.pallas_call(
        kernel,
        out_shape=jax.ShapeDtypeStruct((32, COLS), BF16),
        in_specs=[hbm, hbm, hbm, hbm, pl.BlockSpec(memory_space=pltpu.VMEM)],
        out_specs=pl.BlockSpec(memory_space=pltpu.VMEM),
        scratch_shapes=[
            vmem((2 * MICRO, 2, CHUNKS, CHIPS, ROWS, CW), BF16),
            vmem((SEQ, 3, COLS, COLS), BF16),
            vmem((32, D), BF16),
            vmem((96, 128), F32),
            vmem((2, 512, COLS), BF16),
            vmem((32, D), F32),
            vmem((2, 512, COLS), BF16),
            vmem((3, ROWS, COLS), F32),
            vmem((ROWS, 128), F32),
            vmem((ROWS, 128), F32),
            vmem((3, 8, COLS), F32),
            vmem((3, 16, COLS), F32),
            vmem((SEQ, 8, 128), F32),
            vmem((MICRO, CHUNKS, ROWS, CW), BF16),
            vmem((MICRO, SEQ, 16, 128), BF16),
            vmem((2, MICRO, 16, 128), BF16),
            dma((3,)),
            dma((SEQ,)),
            dma((SEQ,)),
            dma((SEQ,)),
            dma((MICRO,)),
            dma((MICRO,)),
            dma((MICRO,)),
            dma((MICRO, 2, 4, CHUNKS)),
            dma((MICRO,)),
            dma((2, MICRO)),
        ],
        compiler_params=pltpu.CompilerParams(
            collective_id=0, has_side_effects=True, vmem_limit_bytes=56 * 2**20
        ),
        cost_estimate=pl.CostEstimate(flops=4 * 10**9, bytes_accessed=8 * 2**20, transcendentals=10**6),
        name="layers",
    )(hidden, modulation.reshape(96, 128), qkv_weight, stale_cache, patch_of.reshape(1, 32))


def solution(mesh):
    placed = (
        P("cfg", "seq", None),
        P("pipe", None, None),
        P("pipe", None, None, "seq"),
        P("cfg", "pipe", None, None, "seq"),
        P("seq"),
    )
    return jax.shard_map(
        body, mesh=mesh, in_specs=placed, out_specs=P("seq", ("cfg", "pipe")), check_vma=False
    )
```
